256 devices in a mesh: occ: 8 (over x, y_lo), vir: 8 (over z), con: 4 (over y_hi, core).
Axes of the slice: x: 4, y: 4 (y_hi: 2, y_lo: 2; y = y_hi * 2 + y_lo), z: 8, core: 2. Of those that a mesh axis runs over, the one named last changes fastest.
Arguments:
- amplitudes: bfloat16 [4096, 65536], P('occ', ('vir', 'con')), may hold values from -6 to 6
- integrals: bfloat16 [1024, 65536], P('occ', ('vir', 'con')), may hold values from -0.046875 to 0.046875
- occ_irrep: int32 [64], replicated, may hold values from 0 to 7
- ab_irrep: int32 [8], replicated, may hold values from 0 to 7
- cd_irrep: int32 [512], P(('vir', 'con')), may hold values from 0 to 7
Outputs:
- residual: bfloat16 [64, 64, 1024], P('occ', None, ('vir', 'con'))
The draws below stay inside these ranges and needn't reach their ends.
All inputs are finite; a program needn't handle non-finite values.
Results may differ from the reference program's by a relative error of at most 0.0015.
Values may be sent and summed in bfloat16 or wider, within the bound.
No kernel may reach another device: no remote copies, remote signals or barrier semaphores. Data moves between devices by JAX's collectives and lax.ppermute only.
A program may use at most 64 MiB of HBM per device.

```python
import math
import jax
import jax.numpy as jnp
import numpy as np
from jax import lax

TILE = 128
IRREPS = 8
ABT = 8
NO = 64
AB = 1024
CD = 65536


def place_ends(entries, key, least, largest):
    longest = entries.shape.index(max(entries.shape))
    spots = []
    for shift in (0, 1):
        where = [jax.random.randint(jax.random.fold_in(key, axis), (), 0, length) for axis, length in enumerate(entries.shape)]
        where[longest] = (where[longest] + shift) % entries.shape[longest]
        spots.append(tuple(where))
    return entries.at[spots[0]].set(least).at[spots[1]].set(largest)


def shard_levels(rng, dims, shards, smallest, high):
    factor_of, own = 1.0, jax.random.fold_in(rng, 6)
    for position, blocks in shards:
        heights = jnp.exp(jax.random.uniform(jax.random.fold_in(own, position), (blocks,), jnp.float32, smallest / len(shards), high / len(shards)))
        factor_of = factor_of * jnp.repeat(heights, dims[position] // blocks).reshape([-1 if axis == position else 1 for axis in range(len(dims))])
    return factor_of


def rank_table(number_of, lean):
    loads = [(1 << 20) // math.isqrt(rank ** lean) + 1 for rank in range(1, number_of + 1)]
    scale = 1 + sum(loads) // (1 << 30)
    return np.cumsum(np.array([max(1, weight // scale) for weight in loads]))


def ranked_ids(own_key, shape, number_of, lean):
    listing = rank_table(number_of, lean)
    ticket = jax.random.randint(jax.random.fold_in(own_key, 1), shape, 0, int(listing[number_of - 1]))
    standing = jnp.searchsorted(jnp.asarray(listing, jnp.int32), ticket, side="right")
    return jax.random.permutation(jax.random.fold_in(own_key, 2), number_of)[standing].astype(jnp.int32)


def noise(rng, extent, deviation, limit, split=(), held_as=jnp.bfloat16):
    drawn = deviation * jax.random.normal(rng, extent, jnp.float32)
    if split:
        drawn = drawn * shard_levels(rng, extent, split, -0.22, 0.18)
    return jnp.clip(drawn, -limit, limit).astype(held_as)


def setup_inputs(seed: int = 0) -> dict:
    seeds = jax.random.split(jax.random.key(seed), 6)
    return {
        "amplitudes": noise(seeds[0], (NO * NO, CD), 1.0, 6.0, ((0, 8), (1, 32))),
        "integrals": noise(seeds[1], (AB, CD), (CD // 4) ** -0.5, 0.046875, ((0, 8), (1, 32))),
        "occ_irrep": place_ends(ranked_ids(seeds[2], (NO,), IRREPS, 2), jax.random.fold_in(seeds[2], 3), 0, IRREPS - 1).astype(jnp.int32),
        "ab_irrep": place_ends(ranked_ids(seeds[3], (ABT,), IRREPS, 2), jax.random.fold_in(seeds[3], 3), 0, IRREPS - 1).astype(jnp.int32),
        "cd_irrep": place_ends(ranked_ids(seeds[4], (CD // TILE,), IRREPS, 2), jax.random.fold_in(seeds[4], 3), 0, IRREPS - 1).astype(jnp.int32),
    }


def mask_columns(values, row_labels, col_labels):
    return jnp.where(row_labels[:, None] == col_labels[None, :], values, jnp.zeros((), values.dtype))


def reference(amplitudes, integrals, occ_irrep, ab_irrep, cd_irrep):
    pair_irrep = jnp.bitwise_xor(occ_irrep[:, None], occ_irrep[None, :]).astype(jnp.int32)
    col_labels = jnp.repeat(cd_irrep, TILE)
    ab_labels = jnp.repeat(ab_irrep, TILE)
    masked_v = mask_columns(integrals, ab_labels, col_labels)
    slabs = amplitudes.reshape(NO, NO, CD)

    def contract_row(operands):
        slab_rows, labels = operands
        masked_t = mask_columns(slab_rows, labels, col_labels)
        return lax.dot_general(masked_t, masked_v, (((1,), (1,)), ((), ())), preferred_element_type=jnp.float32)

    product = lax.map(contract_row, (slabs, pair_irrep))
    return (2.0 * product - jnp.transpose(product, (1, 0, 2))).astype(jnp.bfloat16)
```

```python
import jax
import jax.numpy as jnp
from jax import lax
from jax.sharding import Mesh, PartitionSpec as P

TILE = 128


def shifted(axis, size, step):
    return lambda a: lax.ppermute(a, axis, [(i, (i + step) % size) for i in range(size)])


def per_device(amplitudes, integrals, occ_irrep, ab_irrep, cd_irrep):
    rows, cols = amplitudes.shape
    orbitals = occ_irrep.shape[0]
    nx, ny = lax.axis_size("x"), lax.axis_size("yl")
    groups = nx * ny
    local = orbitals // groups
    x, y = lax.axis_index("x"), lax.axis_index("yl")
    me = x * ny + y

    partner = shifted("yl", ny, 1)(integrals)
    blocks = [integrals, partner]
    owners = [me, x * ny + (1 - y)]
    for step in range(1, nx):
        move = shifted("x", nx, step)
        for block, other in ((integrals, y), (partner, 1 - y)):
            blocks.append(move(block))
            owners.append(((x - step) % nx) * ny + other)
    owners = jnp.stack(owners)

    mine = lax.dynamic_slice_in_dim(occ_irrep, me * local, local)
    pair = jnp.bitwise_xor(mine[:, None], occ_irrep[None, :]).reshape(rows)
    col = jnp.repeat(cd_irrep, TILE)
    masked_t = jnp.where(pair[:, None] == col[None, :], amplitudes, 0)
    masked_v = [
        jnp.where(ab_irrep[o] == col[None, :], b, 0) for o, b in zip(owners, blocks)
    ]
    slot = jnp.zeros((groups,), jnp.int32).at[owners].set(jnp.arange(groups, dtype=jnp.int32))
    part = lax.dot_general(
        jnp.concatenate(masked_v), masked_t, (((1,), (1,)), ((), ())),
        preferred_element_type=jnp.float32,
    )
    part = part.reshape(groups, 2, 2, TILE // 4, rows)
    part = jnp.take(part, slot, axis=0)

    core = lax.axis_index("core")
    keep = lax.dynamic_index_in_dim(part, core, 2, keepdims=False)
    send = lax.dynamic_index_in_dim(part, 1 - core, 2, keepdims=False)
    part = keep + shifted("core", 2, 1)(send)
    part = part.reshape(groups * 2, TILE // 4, rows)
    part = lax.all_to_all(part, ("vir", "yh"), 0, 0, tiled=True).sum(0)

    own = part.reshape(TILE // 4, local, groups, local).transpose(2, 0, 1, 3)
    got = lax.all_to_all(own, ("x", "yl"), 0, 0, tiled=True)
    own = own.transpose(2, 0, 3, 1)
    got = got.transpose(3, 0, 2, 1)
    out = 2.0 * own - got
    return out.reshape(local, orbitals, TILE // 4).astype(jnp.bfloat16)


def solution(mesh):
    occ, vir, con = (mesh.shape[a] for a in ("occ", "vir", "con"))
    split = Mesh(
        mesh.devices.reshape(occ // 2, 2, vir, 2, con // 2), ("x", "yl", "vir", "yh", "core")
    )
    cd = ("vir", "yh", "core")
    return jax.shard_map(
        per_device,
        mesh=split,
        in_specs=(P(("x", "yl"), cd), P(("x", "yl"), cd), P(), P(), P(cd)),
        out_specs=P(("x", "yl"), None, cd),
        check_vma=False,
    )
```

```python
import functools

import jax
import jax.numpy as jnp
from jax import lax
from jax.experimental import pallas as pl
from jax.experimental.pallas import tpu as pltpu
from jax.sharding import Mesh, PartitionSpec as P

TILE = 128
ROWS = 256
TIERS = (6, 8, 10, 16)
MIB = 1 << 20
SMEM = pl.BlockSpec(memory_space=pltpu.SMEM)
VMEM = pl.BlockSpec(memory_space=pltpu.VMEM)


def shifted(axis, size, step):
    return lambda a: lax.ppermute(a, axis, [(i, (i + step) % size) for i in range(size)])


def params(mib):
    return pltpu.CompilerParams(vmem_limit_bytes=mib * MIB)


def pack_kernel(where, ab, cd, v, tier, *rest):
    outs, count = rest[:-1], rest[-1]
    mine = ab[where[0]]
    for c in range(count.shape[0]):
        count[c] = 0

    @pl.loop(0, cd.shape[0])
    def _(t):
        label = cd[t]
        slot = count[label]
        count[label] = slot + 1

        @pl.when(label == mine)
        def _():
            tile = v[:, pl.ds(pl.multiple_of(t * TILE, TILE), TILE)]
            for out in outs:

                @pl.when(slot < out.shape[1] // TILE)
                def _():
                    out[:, pl.ds(pl.multiple_of(slot * TILE, TILE), TILE)] = tile

    used = count[mine]
    for out in outs:

        @pl.when((used % 2 == 1) & (used < out.shape[1] // TILE))
        def _():
            out[:, pl.ds(pl.multiple_of(used * TILE, TILE), TILE)] = jnp.zeros((v.shape[0], TILE), v.dtype)

    most = count[ab[0]]
    for a in range(1, ab.shape[0]):
        most = jnp.maximum(most, count[ab[a]])
    pick = jnp.int32(0)
    for out in outs[:-1]:
        pick += (most > out.shape[1] // TILE).astype(jnp.int32)
    tier[0] = pick


def pack(where, ab, cd, v):
    return pl.pallas_call(
        pack_kernel,
        out_shape=[jax.ShapeDtypeStruct((1,), jnp.int32)]
        + [jax.ShapeDtypeStruct((v.shape[0], k * TILE), v.dtype) for k in TIERS],
        in_specs=[SMEM, SMEM, SMEM, VMEM],
        out_specs=[SMEM] + [VMEM] * len(TIERS),
        scratch_shapes=[pltpu.SMEM((8,), jnp.int32)],
        compiler_params=params(16),
        name="pack_integrals",
    )(where, ab, cd, v)


def one_hot(shape, spot):
    match = lax.broadcasted_iota(jnp.int32, shape, 0) == spot
    return match.astype(jnp.float32).astype(jnp.bfloat16)


def select_kernel(where, ab, cd, pair, t, out, spots, over, hot, labels, rank, tile_of, count):
    step = pl.program_id(0)
    rows, tiles = t.shape[0], t.shape[1] // TILE
    irreps = count.shape[0]
    me = where[0]

    @pl.when(step == 0)
    def _():
        for c in range(irreps):
            count[c] = 0

        @pl.loop(0, tiles)
        def _(i):
            label = cd[i]
            tile_of[label * tiles + count[label]] = i
            count[label] = count[label] + 1

        label = pair[pl.ds(me, 1), :]
        labels[...] = label
        is_label = lax.broadcasted_iota(jnp.int32, (irreps, rows), 0) == label
        marks = is_label.astype(jnp.float32).astype(jnp.bfloat16)

        @pl.loop(0, rows // TILE)
        def _(k):
            first = pl.multiple_of(k * TILE, TILE)
            shape = (rows, TILE)
            before = lax.broadcasted_iota(jnp.int32, shape, 0) < first + lax.broadcasted_iota(
                jnp.int32, shape, 1
            )
            ahead = jnp.dot(
                marks,
                before.astype(jnp.float32).astype(jnp.bfloat16),
                preferred_element_type=jnp.float32,
            )
            own = lax.broadcasted_iota(jnp.int32, (irreps, TILE), 0) == labels[:, pl.ds(first, TILE)]
            place = jnp.sum(jnp.where(own, ahead, 0.0), axis=0, keepdims=True)
            rank[:, pl.ds(first, TILE)] = place.astype(jnp.int32)

        bad = jnp.int32(0)
        for a in range(ab.shape[0]):
            rows_of = jnp.sum((pair[...] == ab[a]).astype(jnp.int32), axis=1, keepdims=True)
            bad = jnp.maximum(bad, (jnp.max(rows_of) > out.shape[2]).astype(jnp.int32))
        over[0] = bad
        which = lax.broadcasted_iota(jnp.int32, (8, rows), 0)
        place = rank[...]
        values = jnp.where(
            which == 0, label, jnp.where(which == 1, place % 256, jnp.where(which == 2, place // 256, 0))
        )
        values = values.astype(jnp.float32).astype(jnp.bfloat16)
        groups = spots.shape[1] // (2 * TILE)

        @pl.loop(0, 2 * groups)
        def _(k):
            lane = lax.broadcasted_iota(jnp.int32, (1, TILE), 1)
            owner = k % groups
            high, low = (lane // 8) % 8, lane % 8
            i, j = jnp.where(k < groups, high, low), jnp.where(k < groups, low, high)
            source = jnp.where(lane < 64, i * 64 + owner * 8 + j, -1)
            moved = jnp.dot(
                values, one_hot((rows, TILE), source), preferred_element_type=jnp.float32
            ).astype(jnp.int32)
            here = (moved[0:1] == ab[where[1]]) & (lane < 64)
            spots[:, pl.ds(pl.multiple_of(k * TILE, TILE), TILE)] = jnp.where(
                here, moved[1:2] + 256 * moved[2:3], -1
            )

    want = ab[step]
    spot = jnp.where(labels[...] == want, rank[...], -1)
    hot[...] = one_hot(hot.shape, spot)
    used = count[want]

    @pl.loop(0, used)
    def _(s):
        i = tile_of[want * tiles + s]
        piece = t[:, pl.ds(pl.multiple_of(i * TILE, TILE), TILE)]
        rows_in = jnp.dot(hot[...], piece, preferred_element_type=jnp.float32)
        out[0, pl.ds(pl.multiple_of(s * TILE, TILE), TILE), :] = jnp.transpose(rows_in).astype(jnp.bfloat16)

    @pl.when(used % 2 == 1)
    def _():
        out[0, pl.ds(pl.multiple_of(used * TILE, TILE), TILE), :] = jnp.zeros(
            (TILE, out.shape[2]), jnp.bfloat16
        )


def select(slots, where, ab, cd, pair, t):
    abt, tiles, groups = ab.shape[0], t.shape[1] // TILE, pair.shape[0]
    return pl.pallas_call(
        select_kernel,
        grid=(abt,),
        out_shape=[
            jax.ShapeDtypeStruct((abt, slots * TILE, ROWS), t.dtype),
            jax.ShapeDtypeStruct((1, 2 * groups * TILE), jnp.int32),
            jax.ShapeDtypeStruct((1,), jnp.int32),
        ],
        in_specs=[
            SMEM,
            SMEM,
            SMEM,
            pl.BlockSpec(pair.shape, lambda i: (0, 0)),
            pl.BlockSpec(t.shape, lambda i: (0, 0)),
        ],
        out_specs=[
            pl.BlockSpec((1, slots * TILE, ROWS), lambda i: (i, 0, 0)),
            pl.BlockSpec((1, 2 * groups * TILE), lambda i: (0, 0)),
            SMEM,
        ],
        scratch_shapes=[
            pltpu.VMEM((ROWS, t.shape[0]), jnp.bfloat16),
            pltpu.VMEM((1, t.shape[0]), jnp.int32),
            pltpu.VMEM((1, t.shape[0]), jnp.int32),
            pltpu.SMEM((8 * tiles,), jnp.int32),
            pltpu.SMEM((8,), jnp.int32),
        ],
        compiler_params=params(24),
        name="select_amplitudes",
    )(where, ab, cd, pair, t)


def product_kernel(where, owners, ab, cd, t, *rest):
    blocks, (keep, send, acc, count) = rest[:-4], rest[-4:]
    core = where[2]
    part = acc.shape[0] // 4
    for c in range(count.shape[0]):
        count[c] = 0

    @pl.loop(0, cd.shape[0])
    def _(i):
        count[cd[i]] = count[cd[i]] + 1

    for b, block in enumerate(blocks):
        v = owners[b]

        def add(s, total, block=block, v=v):
            span = pl.ds(pl.multiple_of(s * 2 * TILE, 2 * TILE), 2 * TILE)
            return total + jnp.dot(block[:, span], t[v, span, :], preferred_element_type=jnp.float32)

        acc[...] = lax.fori_loop(
            0, (count[ab[v]] + 1) // 2, add, jnp.zeros(acc.shape, jnp.float32)
        )
        for y in range(2):
            for out, c in ((keep, core), (send, 1 - core)):
                first = pl.multiple_of((2 * y + c) * part, part)
                out[v, y] = acc[pl.ds(first, part), :]


def product(where, owners, ab, cd, t, blocks):
    shape = jax.ShapeDtypeStruct((t.shape[0], 2, TILE // 4, t.shape[2]), jnp.float32)
    return pl.pallas_call(
        product_kernel,
        out_shape=[shape, shape],
        in_specs=[SMEM] * 4 + [VMEM] * (1 + len(blocks)),
        out_specs=[VMEM, VMEM],
        scratch_shapes=[pltpu.VMEM((TILE, t.shape[2]), jnp.float32), pltpu.SMEM((8,), jnp.int32)],
        compiler_params=params(32),
        name="product",
    )(where, owners, ab, cd, t, *blocks)


def halve_kernel(where, a, b, keep, send):
    y = where[3]
    for out, half in ((keep, y), (send, 1 - y)):
        for v in range(out.shape[0]):
            out[v] = a[v, half] + b[v, half]


def halve(where, a, b):
    shape = jax.ShapeDtypeStruct((a.shape[0],) + a.shape[2:], jnp.float32)
    return pl.pallas_call(
        halve_kernel,
        out_shape=[shape, shape],
        in_specs=[SMEM, VMEM, VMEM],
        out_specs=[VMEM, VMEM],
        compiler_params=params(16),
        name="halve",
    )(where, a, b)


def spread_kernel(spots, parts, own, send):
    total = parts[0]
    for z in range(1, parts.shape[0]):
        total += parts[z]
    high = total.astype(jnp.bfloat16)
    rest = total - high.astype(jnp.float32)
    middle = rest.astype(jnp.bfloat16)
    low = (rest - middle.astype(jnp.float32)).astype(jnp.bfloat16)
    split = jnp.concatenate([high, middle, low], axis=0)
    n = total.shape[0]
    groups = own.shape[0]

    @pl.loop(0, groups)
    def _(o):
        for out, first in ((own, 0), (send, groups)):
            spot = spots[:, pl.ds(pl.multiple_of((first + o) * TILE, TILE), TILE)]
            hot = one_hot((total.shape[1], TILE), spot)
            x = jnp.dot(split, hot, preferred_element_type=jnp.float32)
            out[o] = x[:n] + (x[n : 2 * n] + x[2 * n :])


def spread(spots, parts):
    shape = jax.ShapeDtypeStruct((spots.shape[1] // (2 * TILE), parts.shape[1], TILE), jnp.float32)
    return pl.pallas_call(
        spread_kernel,
        out_shape=[shape, shape],
        in_specs=[VMEM, VMEM],
        out_specs=[VMEM, VMEM],
        compiler_params=params(16),
        name="spread",
    )(spots, parts)


def finish_kernel(own, got, out, whole):
    local = whole.shape[0]
    for o in range(own.shape[0]):
        x = jnp.transpose(2.0 * own[o] - got[o])
        for i in range(local):
            whole[i, o * 8 : (o + 1) * 8, :] = x[i * 8 : (i + 1) * 8, :]
    out[...] = whole[...].astype(jnp.bfloat16)


def finish(own, got):
    groups, width, _ = own.shape
    return pl.pallas_call(
        finish_kernel,
        out_shape=jax.ShapeDtypeStruct((8, groups * 8, width), jnp.bfloat16),
        in_specs=[VMEM, VMEM],
        out_specs=VMEM,
        scratch_shapes=[pltpu.VMEM((8, groups * 8, width), jnp.float32)],
        compiler_params=params(16),
        name="finish",
    )(own, got)


def gather(v):
    nx, ny = lax.axis_size("x"), lax.axis_size("yl")
    partner = shifted("yl", ny, 1)(v)
    blocks = [v, partner]
    for step in range(1, nx):
        move = shifted("x", nx, step)
        blocks += [move(v), move(partner)]
    return blocks


def owners_of():
    nx, ny = lax.axis_size("x"), lax.axis_size("yl")
    x, y = lax.axis_index("x"), lax.axis_index("yl")
    owners = []
    for step in range(nx):
        first = ((x - step) % nx) * ny
        owners += [first + y, first + 1 - y]
    return jnp.stack(owners).astype(jnp.int32)


def dense(amplitudes, integrals, occ_irrep, ab_irrep, cd_irrep):
    rows, cols = amplitudes.shape
    orbitals = occ_irrep.shape[0]
    groups = lax.axis_size("x") * lax.axis_size("yl")
    local = orbitals // groups
    me = lax.axis_index("x") * lax.axis_size("yl") + lax.axis_index("yl")
    owners = owners_of()
    blocks = gather(integrals)
    mine = lax.dynamic_slice_in_dim(occ_irrep, me * local, local)
    pair = jnp.bitwise_xor(mine[:, None], occ_irrep[None, :]).reshape(rows)
    col = jnp.repeat(cd_irrep, TILE)
    masked_t = jnp.where(pair[:, None] == col[None, :], amplitudes, 0)
    masked_v = [jnp.where(ab_irrep[owners[k]] == col[None, :], b, 0) for k, b in enumerate(blocks)]
    part = lax.dot_general(
        jnp.concatenate(masked_v), masked_t, (((1,), (1,)), ((), ())), preferred_element_type=jnp.float32
    )
    part = jnp.zeros_like(part).reshape(groups, TILE, rows).at[owners].set(part.reshape(groups, TILE, rows))
    part = part.reshape(groups, 2, 2, TILE // 4, rows)
    core = lax.axis_index("core")
    keep = lax.dynamic_index_in_dim(part, core, 2, keepdims=False)
    send = lax.dynamic_index_in_dim(part, 1 - core, 2, keepdims=False)
    part = (keep + shifted("core", 2, 1)(send)).reshape(groups * 2, TILE // 4, rows)
    part = lax.all_to_all(part, ("vir", "yh"), 0, 0, tiled=True).sum(0)
    own = part.reshape(TILE // 4, local, groups, local).transpose(2, 0, 1, 3)
    got = lax.all_to_all(own, ("x", "yl"), 0, 0, tiled=True)
    out = 2.0 * own.transpose(2, 0, 3, 1) - got.transpose(3, 0, 2, 1)
    return out.reshape(local, orbitals, TILE // 4).astype(jnp.bfloat16)


def per_device(amplitudes, integrals, occ_irrep, ab_irrep, cd_irrep):
    groups = lax.axis_size("x") * lax.axis_size("yl")
    me = lax.axis_index("x") * lax.axis_size("yl") + lax.axis_index("yl")
    where = jnp.stack(
        [me, lax.axis_index("vir"), lax.axis_index("core"), lax.axis_index("yh")]
    ).astype(jnp.int32)
    tier, *packed = pack(where, ab_irrep, cd_irrep, integrals)

    def partial_sums(slots):
        def run(v, t, occ):
            blocks = gather(v)
            pair = jnp.bitwise_xor(occ.reshape(groups, -1, 1), occ[None, None, :])
            selected, spots, over = select(
                slots, where, ab_irrep, cd_irrep, pair.reshape(groups, t.shape[0]), t
            )
            keep, send = product(where, owners_of(), ab_irrep, cd_irrep, selected, blocks)
            return keep, send, spots, over

        return run

    branches = [
        lambda *a, k=k, n=n: partial_sums(k)(a[n], a[-2], a[-1]) for n, k in enumerate(TIERS)
    ]
    keep, send, spots, over = lax.switch(tier[0], branches, *packed, amplitudes, occ_irrep)
    keep, send = halve(where, keep, shifted("core", 2, 1)(send))
    part = keep + shifted("yh", 2, 1)(send)
    part = lax.all_to_all(part, "vir", 0, 0, tiled=True)
    own, send = spread(spots, part)
    got = lax.all_to_all(send, ("x", "yl"), 0, 0, tiled=True)
    out = finish(own, got)
    args = (amplitudes, integrals, occ_irrep, ab_irrep, cd_irrep)
    return lax.cond(over[0] > 0, lambda out, *a: dense(*a), lambda out, *a: out, out, *args)


def solution(mesh):
    occ, vir, con = (mesh.shape[a] for a in ("occ", "vir", "con"))
    split = Mesh(
        mesh.devices.reshape(occ // 2, 2, vir, 2, con // 2), ("x", "yl", "vir", "yh", "core")
    )
    cd = ("vir", "yh", "core")
    return jax.shard_map(
        per_device,
        mesh=split,
        in_specs=(P(("x", "yl"), cd), P(("x", "yl"), cd), P(), P(), P(cd)),
        out_specs=P(("x", "yl"), None, cd),
        check_vma=False,
    )
```

```python
import functools

import jax
import jax.numpy as jnp
from jax import lax
from jax.experimental import pallas as pl
from jax.experimental.pallas import tpu as pltpu
from jax.sharding import Mesh, PartitionSpec as P

TILE = 128
ROWS = 256
SCALES = 8
STEP = 2.0**14
FIRST = 10
DIRECT = 6
MIB = 1 << 20
SMEM = pl.BlockSpec(memory_space=pltpu.SMEM)
VMEM = pl.BlockSpec(memory_space=pltpu.VMEM)
ANY = pl.BlockSpec(memory_space=pl.ANY)


def shifted(axis, size, step):
    return lambda a: lax.ppermute(a, axis, [(i, (i + step) % size) for i in range(size)])


def cost(us):
    return pl.CostEstimate(flops=int(us * 1.1e9), bytes_accessed=0, transcendentals=0)


def params(mib):
    return pltpu.CompilerParams(vmem_limit_bytes=mib * MIB)


def pack_kernel(skip, where, ab, cd, v, more, out, count):
    slots = out.shape[1] // TILE
    mine = ab[where[0]]
    for c in range(count.shape[0]):
        count[c] = 0

    @pl.loop(0, cd.shape[0])
    def _(t):
        label = cd[t]
        slot = count[label] - skip
        count[label] = count[label] + 1

        @pl.when((label == mine) & (slot >= 0) & (slot < slots))
        def _():
            out[:, pl.ds(pl.multiple_of(slot * TILE, TILE), TILE)] = v[
                :, pl.ds(pl.multiple_of(t * TILE, TILE), TILE)
            ]

    @pl.loop(jnp.clip(count[mine] - skip, 0, slots), slots)
    def _(slot):
        out[:, pl.ds(pl.multiple_of(slot * TILE, TILE), TILE)] = jnp.zeros((v.shape[0], TILE), v.dtype)

    most = count[ab[0]]
    for a in range(1, ab.shape[0]):
        most = jnp.maximum(most, count[ab[a]])
    more[0] = (most > skip + slots).astype(jnp.int32)


def pack(skip, slots, where, ab, cd, v):
    return pl.pallas_call(
        functools.partial(pack_kernel, skip),
        out_shape=[
            jax.ShapeDtypeStruct((1,), jnp.int32),
            jax.ShapeDtypeStruct((v.shape[0], slots * TILE), v.dtype),
        ],
        in_specs=[SMEM, SMEM, SMEM, VMEM],
        out_specs=[SMEM, VMEM],
        scratch_shapes=[pltpu.SMEM((8,), jnp.int32)],
        compiler_params=params(4),
        cost_estimate=cost(2.0),
        name="pack_integrals",
    )(where, ab, cd, v)


def one_hot(shape, spot):
    match = lax.broadcasted_iota(jnp.int32, shape, 0) == spot
    return match.astype(jnp.float32).astype(jnp.bfloat16)


def rank_kernel(where, occ, ab, occ_row, labels, rank, spots, over):
    orbitals, rows = occ_row.shape[1], labels.shape[1]
    local = rows // orbitals
    irreps, abt = 8, ab.shape[0]
    me, mine = where[0], ab[where[1]]
    for i in range(local):
        labels[:, i * orbitals : (i + 1) * orbitals] = occ_row[...] ^ occ[me * local + i]

    label = labels[...]
    is_label = lax.broadcasted_iota(jnp.int32, (irreps, rows), 0) == label
    marks = is_label.astype(jnp.float32).astype(jnp.bfloat16)

    @pl.loop(0, rows // TILE)
    def _(k):
        first = pl.multiple_of(k * TILE, TILE)
        shape = (rows, TILE)
        before = lax.broadcasted_iota(jnp.int32, shape, 0) < first + lax.broadcasted_iota(
            jnp.int32, shape, 1
        )
        ahead = jnp.dot(
            marks, before.astype(jnp.float32).astype(jnp.bfloat16), preferred_element_type=jnp.float32
        )
        own = lax.broadcasted_iota(jnp.int32, (irreps, TILE), 0) == labels[:, pl.ds(first, TILE)]
        rank[:, pl.ds(first, TILE)] = jnp.sum(
            jnp.where(own, ahead, 0.0), axis=0, keepdims=True
        ).astype(jnp.int32)

    column = lax.broadcasted_iota(jnp.int32, (abt, orbitals), 0)
    partner = occ_row[...]
    want = jnp.zeros((abt, orbitals), jnp.int32)
    for v in range(abt):
        want = jnp.where(column == v, ab[v], want)
    want = want ^ partner
    of_irrep = lax.broadcasted_iota(jnp.int32, (irreps, orbitals), 0) == partner
    count = jnp.sum(of_irrep.astype(jnp.float32), axis=1, keepdims=True)
    met = jnp.zeros((abt, orbitals), jnp.float32)
    for c in range(irreps):
        met = jnp.where(want == c, count[c : c + 1, :], met)
    shape = (orbitals, TILE)
    group = lax.broadcasted_iota(jnp.int32, shape, 0) // local == lax.broadcasted_iota(jnp.int32, shape, 1)
    held = jnp.dot(
        met.astype(jnp.bfloat16),
        group.astype(jnp.float32).astype(jnp.bfloat16),
        preferred_element_type=jnp.float32,
    )
    over[0] = (jnp.max(held) > ROWS - SCALES).astype(jnp.int32)

    which = lax.broadcasted_iota(jnp.int32, (8, rows), 0)
    place = rank[...]
    values = jnp.where(
        which == 0, label, jnp.where(which == 1, place % 256, jnp.where(which == 2, place // 256, 0))
    )
    values = values.astype(jnp.float32).astype(jnp.bfloat16)

    @pl.loop(0, spots.shape[1] // TILE)
    def _(owner):
        lane = lax.broadcasted_iota(jnp.int32, (1, TILE), 1)
        j, i = lane // local, lane % local
        source = jnp.where(j < local, i * orbitals + owner * local + j, -1)
        moved = jnp.dot(
            values, one_hot((rows, TILE), source), preferred_element_type=jnp.float32
        ).astype(jnp.int32)
        here = (moved[0:1] == mine) & (j < local)
        spots[:, pl.ds(pl.multiple_of(owner * TILE, TILE), TILE)] = jnp.where(
            here, moved[1:2] + 256 * moved[2:3], -1
        )


def ranks(where, occ, ab, rows, groups):
    return pl.pallas_call(
        rank_kernel,
        out_shape=[
            jax.ShapeDtypeStruct((1, rows), jnp.int32),
            jax.ShapeDtypeStruct((1, rows), jnp.int32),
            jax.ShapeDtypeStruct((1, groups * TILE), jnp.int32),
            jax.ShapeDtypeStruct((1,), jnp.int32),
        ],
        in_specs=[SMEM, SMEM, SMEM, VMEM],
        out_specs=[VMEM, VMEM, VMEM, SMEM],
        compiler_params=params(4),
        cost_estimate=cost(3.3),
        name="ranks",
    )(where, occ, ab, occ.reshape(1, -1))


def select_kernel(skip, after, ab, cd, labels, rank, t, *rest):
    out, hot, tile_of, count = rest[after:]
    tiles, slots = cd.shape[0], out.shape[1] // TILE
    for c in range(count.shape[0]):
        count[c] = 0

    @pl.loop(0, tiles)
    def _(i):
        label = cd[i]
        tile_of[label * tiles + count[label]] = i
        count[label] = count[label] + 1

    @pl.loop(0, ab.shape[0])
    def _(v):
        want = ab[v]

        @pl.when(first_of(ab, v) == v)
        def _():
            hot[...] = one_hot(hot.shape, jnp.where(labels[...] == want, rank[...], -1))
            used = jnp.clip(count[want] - skip, 0, slots)

            @pl.loop(0, used)
            def _(s):
                i = tile_of[want * tiles + skip + s]
                piece = t[:, pl.ds(pl.multiple_of(i * TILE, TILE), TILE)]
                rows_in = jnp.dot(hot[...], piece, preferred_element_type=jnp.float32)
                out[v, pl.ds(pl.multiple_of(s * TILE, TILE), TILE), :] = jnp.transpose(rows_in).astype(
                    jnp.bfloat16
                )

            @pl.loop(used, slots)
            def _(s):
                out[v, pl.ds(pl.multiple_of(s * TILE, TILE), TILE), :] = jnp.zeros(
                    (TILE, out.shape[2]), jnp.bfloat16
                )


def first_of(ab, v):
    want = ab[v]
    first = jnp.int32(0)
    for a in reversed(range(ab.shape[0])):
        first = jnp.where(ab[a] == want, a, first)
    return first


def select(skip, slots, ab, cd, labels, rank, t, after):
    return pl.pallas_call(
        functools.partial(select_kernel, skip, len(after)),
        out_shape=jax.ShapeDtypeStruct((ab.shape[0], slots * TILE, ROWS), t.dtype),
        in_specs=[SMEM, SMEM, VMEM, VMEM, VMEM] + [ANY] * len(after),
        out_specs=VMEM,
        scratch_shapes=[
            pltpu.VMEM((ROWS, t.shape[0]), jnp.bfloat16),
            pltpu.SMEM((8 * cd.shape[0],), jnp.int32),
            pltpu.SMEM((8,), jnp.int32),
        ],
        compiler_params=params(12),
        cost_estimate=cost(5.0),
        name="select_amplitudes",
    )(ab, cd, labels, rank, t, *after)


def product_kernel(sizes, where, owners, ab, t, *rest):
    pieces, (keep, send, largest, acc) = list(rest[:-4]), rest[-4:]
    core = where[2]
    part = acc.shape[0] // 4
    most = jnp.zeros((8, acc.shape[1]), jnp.float32)
    for b, size in enumerate(sizes):
        v = owners[b]
        f = first_of(ab, v)
        first = 0
        for k in range(size):
            piece = pieces.pop(0)
            last = first + piece.shape[1]
            x = jnp.dot(piece[...], t[f, first:last, :], preferred_element_type=jnp.float32)
            acc[...] = x if k == 0 else acc[...] + x
            first = last
        most = jnp.maximum(most, jnp.max(jnp.abs(acc[...]).reshape(-1, 8, acc.shape[1]), axis=0))
        for y in range(2):
            for out, c in ((keep, core), (send, 1 - core)):
                row = pl.multiple_of((2 * y + c) * part, part)
                out[v, y] = acc[pl.ds(row, part), :]
    largest[...] = jnp.full(largest.shape, jnp.max(most), jnp.float32)


def product(where, owners, ab, t, blocks):
    shape = jax.ShapeDtypeStruct((t.shape[0], 2, TILE // 4, t.shape[2]), jnp.float32)
    pieces = [piece for block in blocks for piece in block]
    return pl.pallas_call(
        functools.partial(product_kernel, [len(block) for block in blocks]),
        out_shape=[shape, shape, jax.ShapeDtypeStruct((8, TILE), jnp.float32)],
        in_specs=[SMEM] * 3 + [VMEM] * (1 + len(pieces)),
        out_specs=[VMEM, VMEM, VMEM],
        scratch_shapes=[pltpu.VMEM((TILE, t.shape[2]), jnp.float32)],
        compiler_params=params(12),
        cost_estimate=cost(2.5),
        name="product",
    )(where, owners, ab, t, *pieces)


def combine_kernel(keep, got, a, b, out):
    top = (a[...] + b[...])[0:1, :]
    up, down = jnp.ones_like(top), jnp.ones_like(top)
    for bits in (64, 32, 8, 4, 2, 1):
        fits = top * (up * 2.0**bits) <= 2.0**15
        up = jnp.where(fits, up * 2.0**bits, up)
        down = jnp.where(fits, down * 2.0**-bits, down)
    lane = lax.broadcasted_iota(jnp.int32, top.shape, 1)
    parts = jnp.zeros_like(top)
    for i in range(SCALES):
        parts = jnp.where(lane == TILE - SCALES + i, jnp.maximum(down, 1.0 / STEP), parts)
        down = jnp.where(down < 1.0 / STEP, down * STEP, 1.0)
    up = jnp.concatenate([up, jnp.where(lane < TILE - SCALES, up, 0.0)], axis=1)
    parts = jnp.concatenate([jnp.zeros_like(top), parts], axis=1)
    for v in range(keep.shape[0]):
        for y in range(keep.shape[1]):
            out[v * keep.shape[1] + y] = (keep[v, y] + got[v, y]) * up + parts


def combine(keep, got, a, b):
    return pl.pallas_call(
        combine_kernel,
        out_shape=jax.ShapeDtypeStruct((keep.shape[0] * keep.shape[1],) + keep.shape[2:], jnp.float32),
        in_specs=[VMEM] * 4,
        out_specs=VMEM,
        compiler_params=params(6),
        cost_estimate=cost(1.2),
        name="combine",
    )(keep, got, a, b)


def spread_kernel(where, ab, labels, rank, spots, parts, own, send):
    total = jnp.zeros(parts.shape[1:], jnp.float32)
    for z in range(parts.shape[0]):
        part = parts[z]
        down = part[0:1, ROWS - SCALES : ROWS - SCALES + 1]
        for i in range(1, SCALES):
            down *= part[0:1, ROWS - SCALES + i : ROWS - SCALES + i + 1]
        total += part * down
    high = total.astype(jnp.bfloat16)
    rest = total - high.astype(jnp.float32)
    middle = rest.astype(jnp.bfloat16)
    low = (rest - middle.astype(jnp.float32)).astype(jnp.bfloat16)
    split = jnp.concatenate([high, middle, low], axis=0)
    n = total.shape[0]

    def placed(spot):
        x = jnp.dot(split, one_hot((total.shape[1], spot.shape[1]), spot), preferred_element_type=jnp.float32)
        return x[:n] + (x[n : 2 * n] + x[2 * n :])

    for o in range(0, send.shape[0], 2):
        x = placed(spots[:, o * TILE : (o + 2) * TILE])
        send[o] = x[:, :TILE]
        send[o + 1] = x[:, TILE:]
    mine = ab[where[1]]
    for k in range(0, own.shape[1], 2 * TILE):
        span = slice(k, k + 2 * TILE)
        own[:, span] = placed(jnp.where(labels[:, span] == mine, rank[:, span], -1))


def spread(where, ab, labels, rank, spots, parts):
    return pl.pallas_call(
        spread_kernel,
        out_shape=[
            jax.ShapeDtypeStruct((parts.shape[1], labels.shape[1]), jnp.float32),
            jax.ShapeDtypeStruct((spots.shape[1] // TILE, parts.shape[1], TILE), jnp.float32),
        ],
        in_specs=[SMEM, SMEM] + [VMEM] * 4,
        out_specs=[VMEM, VMEM],
        compiler_params=params(6),
        cost_estimate=cost(1.7),
        name="spread",
    )(where, ab, labels, rank, spots, parts)


def finish_kernel(own, got, out, turned):
    local, orbitals, width = turned.shape
    for o in range(got.shape[0]):
        x = jnp.transpose(got[o])
        for i in range(local):
            turned[i, o * local : (o + 1) * local, :] = x[i * local : (i + 1) * local, :]
    for i in range(local):
        mine = own[:, i * orbitals : (i + 1) * orbitals]
        out[i * width : (i + 1) * width, :] = (2.0 * mine - jnp.transpose(turned[i])).astype(jnp.bfloat16)


def finish(own, got, local, orbitals):
    width = own.shape[0]
    return pl.pallas_call(
        finish_kernel,
        out_shape=jax.ShapeDtypeStruct((local * width, orbitals), jnp.bfloat16),
        in_specs=[VMEM, VMEM],
        out_specs=VMEM,
        scratch_shapes=[pltpu.VMEM((local, orbitals, width), jnp.float32)],
        compiler_params=params(4),
        cost_estimate=cost(0.4),
        name="finish",
    )(own, got)


def take_kernel(first, v, after, out):
    out[...] = v[:, first : first + out.shape[1]]


def take(v, first, last, after):
    return pl.pallas_call(
        functools.partial(take_kernel, first),
        out_shape=jax.ShapeDtypeStruct((v.shape[0], last - first), v.dtype),
        in_specs=[VMEM, ANY],
        out_specs=VMEM,
        compiler_params=params(4),
        name="take",
    )(v, after)


def gather(v, direct, after):
    nx, ny = lax.axis_size("x"), lax.axis_size("yl")
    swap = shifted("yl", ny, 1)
    moves = [shifted("x", nx, step) for step in range(1, nx)]
    partner = swap(v)
    own = [move(v) for move in moves]
    head = take(partner, 0, direct * TILE, after)
    blocks = [[v], [partner]]
    for move, block in zip(moves, own, strict=True):
        blocks += [[block], [move(head)]]
    tails = []
    if direct * TILE < v.shape[1]:
        for k, block in enumerate(own):
            tails.append(take(block, direct * TILE, v.shape[1], head))
            blocks[2 * k + 3].append(swap(tails[-1]))
    return blocks, tails


def owners_of():
    nx, ny = lax.axis_size("x"), lax.axis_size("yl")
    x, y = lax.axis_index("x"), lax.axis_index("yl")
    owners = []
    for step in range(nx):
        first = ((x - step) % nx) * ny
        owners += [first + y, first + 1 - y]
    return jnp.stack(owners).astype(jnp.int32)


def dense(amplitudes, integrals, occ_irrep, ab_irrep, cd_irrep):
    rows, cols = amplitudes.shape
    orbitals = occ_irrep.shape[0]
    groups = lax.axis_size("x") * lax.axis_size("yl")
    local = orbitals // groups
    me = lax.axis_index("x") * lax.axis_size("yl") + lax.axis_index("yl")
    blocks = lax.all_to_all(
        jnp.broadcast_to(integrals, (groups,) + integrals.shape), ("x", "yl"), 0, 0, tiled=True
    )
    mine = lax.dynamic_slice_in_dim(occ_irrep, me * local, local)
    pair = jnp.bitwise_xor(mine[:, None], occ_irrep[None, :]).reshape(rows)
    col = jnp.repeat(cd_irrep, TILE)
    masked_t = jnp.where(pair[:, None] == col[None, :], amplitudes, 0)
    masked_v = jnp.where(ab_irrep[:, None, None] == col[None, None, :], blocks, 0)
    part = lax.dot_general(
        masked_v.reshape(-1, cols), masked_t, (((1,), (1,)), ((), ())), preferred_element_type=jnp.float32
    )
    part = part.reshape(groups * 4, TILE // 4, rows)
    part = lax.all_to_all(part, ("vir", "yh", "core"), 0, 0, tiled=True).sum(0)
    own = part.reshape(TILE // 4, local, groups, local).transpose(2, 0, 1, 3)
    got = lax.all_to_all(own, ("x", "yl"), 0, 0, tiled=True)
    out = 2.0 * own.transpose(2, 0, 3, 1) - got.transpose(3, 0, 2, 1)
    return out.reshape(local, orbitals, TILE // 4).astype(jnp.bfloat16)


def per_device(amplitudes, integrals, occ_irrep, ab_irrep, cd_irrep):
    groups = lax.axis_size("x") * lax.axis_size("yl")
    orbitals = occ_irrep.shape[0]
    rows = amplitudes.shape[0]
    me = lax.axis_index("x") * lax.axis_size("yl") + lax.axis_index("yl")
    where = jnp.stack([me, lax.axis_index("vir"), lax.axis_index("core")]).astype(jnp.int32)
    owners = owners_of()
    tiles = cd_irrep.shape[0]

    def partial_sums(skip, slots, direct, found, packed):
        blocks, tails = gather(packed, direct, found[1])
        selected = select(skip, slots, ab_irrep, cd_irrep, *found[:2], amplitudes, tails)
        return product(where, owners, ab_irrep, selected, blocks)

    more, packed = pack(0, FIRST, where, ab_irrep, cd_irrep, integrals)
    found = ranks(where, occ_irrep, ab_irrep, rows, groups)
    sums = partial_sums(0, FIRST, DIRECT, found, packed)

    def rest(sums, v, found):
        _, packed = pack(FIRST, tiles - FIRST, where, ab_irrep, cd_irrep, v)
        added = partial_sums(FIRST, tiles - FIRST, tiles - FIRST, found, packed)
        return jax.tree.map(jnp.add, list(sums), list(added))

    keep, send, largest = lax.cond(
        more[0] > 0, rest, lambda sums, v, found: list(sums), list(sums), integrals, found
    )
    labels, rank, spots, over = found
    other = shifted("core", 2, 1)
    part = combine(keep, other(send), largest, other(largest)).astype(jnp.float16)
    part = lax.all_to_all(part, ("vir", "yh"), 0, 0, tiled=True).astype(jnp.float32)
    own, send = spread(where, ab_irrep, labels, rank, spots, part)
    got = lax.all_to_all(send, ("x", "yl"), 0, 0, tiled=True)
    out = lax.cond(
        over[0] > 0,
        lambda own, got, *a: jnp.swapaxes(dense(*a), 1, 2).reshape(-1, orbitals),
        lambda own, got, *a: finish(own, got, rows // orbitals, orbitals),
        *(own, got, amplitudes, integrals, occ_irrep, ab_irrep, cd_irrep),
    )
    return jnp.swapaxes(out.reshape(rows // orbitals, -1, orbitals), 1, 2)


def solution(mesh):
    occ, vir, con = (mesh.shape[a] for a in ("occ", "vir", "con"))
    split = Mesh(
        mesh.devices.reshape(occ // 2, 2, vir, 2, con // 2), ("x", "yl", "vir", "yh", "core")
    )
    cd = ("vir", "yh", "core")
    return jax.shard_map(
        per_device,
        mesh=split,
        in_specs=(P(("x", "yl"), cd), P(("x", "yl"), cd), P(), P(), P(cd)),
        out_specs=P(("x", "yl"), None, cd),
        check_vma=False,
    )
```

```python
import functools

import jax
import jax.numpy as jnp
from jax import lax
from jax.experimental import pallas as pl
from jax.experimental.pallas import tpu as pltpu
from jax.sharding import Mesh, PartitionSpec as P

TILE = 128
ROWS = 256
SCALES = 8
STEP = 2.0**14
FIRST = (6, 4)
MIB = 1 << 20
SMEM = pl.BlockSpec(memory_space=pltpu.SMEM)
VMEM = pl.BlockSpec(memory_space=pltpu.VMEM)
ANY = pl.BlockSpec(memory_space=pl.ANY)


def shifted(axis, size, step):
    return lambda a: lax.ppermute(a, axis, [(i, (i + step) % size) for i in range(size)])


def cost(us):
    return pl.CostEstimate(flops=int(us * 1.1e9), bytes_accessed=0, transcendentals=0)


def params(mib):
    return pltpu.CompilerParams(vmem_limit_bytes=mib * MIB)


def pack_kernel(skip, where, ab, cd, v, more, *rest):
    outs, count = rest[:-1], rest[-1]
    mine = ab[where[0]]
    for c in range(count.shape[0]):
        count[c] = 0

    @pl.loop(0, cd.shape[0])
    def _(t):
        label = cd[t]
        slot = count[label] - skip
        count[label] = count[label] + 1

        @pl.when(label == mine)
        def _():
            tile = v[:, pl.ds(pl.multiple_of(t * TILE, TILE), TILE)]
            first = 0
            for out in outs:
                place = slot - first
                slots = out.shape[1] // TILE

                @pl.when((place >= 0) & (place < slots))
                def _():
                    out[:, pl.ds(pl.multiple_of(place * TILE, TILE), TILE)] = tile

                first += slots

    first = skip
    for out in outs:
        slots = out.shape[1] // TILE

        @pl.loop(jnp.clip(count[mine] - first, 0, slots), slots)
        def _(slot):
            out[:, pl.ds(pl.multiple_of(slot * TILE, TILE), TILE)] = jnp.zeros((v.shape[0], TILE), v.dtype)

        first += slots
    most = count[ab[0]]
    for a in range(1, ab.shape[0]):
        most = jnp.maximum(most, count[ab[a]])
    more[0] = (most > first).astype(jnp.int32)


def pack(skip, pieces, where, ab, cd, v):
    return pl.pallas_call(
        functools.partial(pack_kernel, skip),
        out_shape=[jax.ShapeDtypeStruct((1,), jnp.int32)]
        + [jax.ShapeDtypeStruct((v.shape[0], slots * TILE), v.dtype) for slots in pieces],
        in_specs=[SMEM, SMEM, SMEM, VMEM],
        out_specs=[SMEM] + [VMEM] * len(pieces),
        scratch_shapes=[pltpu.SMEM((8,), jnp.int32)],
        compiler_params=params(4),
        cost_estimate=cost(2.0),
        name="pack_integrals",
    )(where, ab, cd, v)


def one_hot(shape, spot):
    match = lax.broadcasted_iota(jnp.int32, shape, 0) == spot
    return match.astype(jnp.float32).astype(jnp.bfloat16)


def rank_kernel(after, where, occ, ab, occ_row, *rest):
    labels, rank, spots, over = rest[after:]
    orbitals, rows = occ_row.shape[1], labels.shape[1]
    local = rows // orbitals
    irreps, abt = 8, ab.shape[0]
    me, mine = where[0], ab[where[1]]
    for i in range(local):
        labels[:, i * orbitals : (i + 1) * orbitals] = occ_row[...] ^ occ[me * local + i]

    label = labels[...]
    is_label = lax.broadcasted_iota(jnp.int32, (irreps, rows), 0) == label
    marks = is_label.astype(jnp.float32).astype(jnp.bfloat16)

    @pl.loop(0, rows // TILE)
    def _(k):
        first = pl.multiple_of(k * TILE, TILE)
        shape = (rows, TILE)
        before = lax.broadcasted_iota(jnp.int32, shape, 0) < first + lax.broadcasted_iota(
            jnp.int32, shape, 1
        )
        ahead = jnp.dot(
            marks, before.astype(jnp.float32).astype(jnp.bfloat16), preferred_element_type=jnp.float32
        )
        own = lax.broadcasted_iota(jnp.int32, (irreps, TILE), 0) == labels[:, pl.ds(first, TILE)]
        rank[:, pl.ds(first, TILE)] = jnp.sum(
            jnp.where(own, ahead, 0.0), axis=0, keepdims=True
        ).astype(jnp.int32)

    column = lax.broadcasted_iota(jnp.int32, (abt, orbitals), 0)
    partner = occ_row[...]
    want = jnp.zeros((abt, orbitals), jnp.int32)
    for v in range(abt):
        want = jnp.where(column == v, ab[v], want)
    want = want ^ partner
    of_irrep = lax.broadcasted_iota(jnp.int32, (irreps, orbitals), 0) == partner
    count = jnp.sum(of_irrep.astype(jnp.float32), axis=1, keepdims=True)
    met = jnp.zeros((abt, orbitals), jnp.float32)
    for c in range(irreps):
        met = jnp.where(want == c, count[c : c + 1, :], met)
    shape = (orbitals, TILE)
    group = lax.broadcasted_iota(jnp.int32, shape, 0) // local == lax.broadcasted_iota(jnp.int32, shape, 1)
    held = jnp.dot(
        met.astype(jnp.bfloat16),
        group.astype(jnp.float32).astype(jnp.bfloat16),
        preferred_element_type=jnp.float32,
    )
    over[0] = (jnp.max(held) > ROWS - SCALES).astype(jnp.int32)

    which = lax.broadcasted_iota(jnp.int32, (8, rows), 0)
    place = rank[...]
    values = jnp.where(
        which == 0, label, jnp.where(which == 1, place % 256, jnp.where(which == 2, place // 256, 0))
    )
    values = values.astype(jnp.float32).astype(jnp.bfloat16)

    @pl.loop(0, spots.shape[1] // TILE)
    def _(owner):
        lane = lax.broadcasted_iota(jnp.int32, (1, TILE), 1)
        j, i = lane // local, lane % local
        source = jnp.where(j < local, i * orbitals + owner * local + j, -1)
        moved = jnp.dot(
            values, one_hot((rows, TILE), source), preferred_element_type=jnp.float32
        ).astype(jnp.int32)
        here = (moved[0:1] == mine) & (j < local)
        spots[:, pl.ds(pl.multiple_of(owner * TILE, TILE), TILE)] = jnp.where(
            here, moved[1:2] + 256 * moved[2:3], -1
        )


def ranks(where, occ, ab, rows, groups, after):
    return pl.pallas_call(
        functools.partial(rank_kernel, len(after)),
        out_shape=[
            jax.ShapeDtypeStruct((1, rows), jnp.int32),
            jax.ShapeDtypeStruct((1, rows), jnp.int32),
            jax.ShapeDtypeStruct((1, groups * TILE), jnp.int32),
            jax.ShapeDtypeStruct((1,), jnp.int32),
        ],
        in_specs=[SMEM, SMEM, SMEM, VMEM] + [ANY] * len(after),
        out_specs=[VMEM, VMEM, VMEM, SMEM],
        compiler_params=params(4),
        cost_estimate=cost(3.3),
        name="ranks",
    )(where, occ, ab, occ.reshape(1, -1), *after)


def select_kernel(skip, after, ab, cd, labels, rank, t, *rest):
    out, hot, tile_of, count = rest[after:]
    tiles, slots = cd.shape[0], out.shape[1] // TILE
    for c in range(count.shape[0]):
        count[c] = 0

    @pl.loop(0, tiles)
    def _(i):
        label = cd[i]
        tile_of[label * tiles + count[label]] = i
        count[label] = count[label] + 1

    @pl.loop(0, ab.shape[0])
    def _(v):
        want = ab[v]

        @pl.when(first_of(ab, v) == v)
        def _():
            hot[...] = one_hot(hot.shape, jnp.where(labels[...] == want, rank[...], -1))
            used = jnp.clip(count[want] - skip, 0, slots)

            @pl.loop(0, (used + 1) // 2)
            def _(s):
                spans = []
                for k in range(2):
                    i = tile_of[jnp.minimum(want * tiles + skip + 2 * s + k, want * tiles + skip + used - 1)]
                    spans.append(t[:, pl.ds(pl.multiple_of(i * TILE, TILE), TILE)])
                rows_in = jnp.dot(hot[...], jnp.concatenate(spans, axis=1), preferred_element_type=jnp.float32)
                out[v, pl.ds(pl.multiple_of(s * 2 * TILE, 2 * TILE), 2 * TILE), :] = jnp.transpose(
                    rows_in
                ).astype(jnp.bfloat16)

            @pl.loop(2 * ((used + 1) // 2), slots)
            def _(s):
                out[v, pl.ds(pl.multiple_of(s * TILE, TILE), TILE), :] = jnp.zeros(
                    (TILE, out.shape[2]), jnp.bfloat16
                )


def first_of(ab, v):
    want = ab[v]
    first = jnp.int32(0)
    for a in reversed(range(ab.shape[0])):
        first = jnp.where(ab[a] == want, a, first)
    return first


def select(skip, slots, ab, cd, labels, rank, t, after):
    return pl.pallas_call(
        functools.partial(select_kernel, skip, len(after)),
        out_shape=jax.ShapeDtypeStruct((ab.shape[0], slots * TILE, ROWS), t.dtype),
        in_specs=[SMEM, SMEM, VMEM, VMEM, VMEM] + [ANY] * len(after),
        out_specs=VMEM,
        scratch_shapes=[
            pltpu.VMEM((ROWS, t.shape[0]), jnp.bfloat16),
            pltpu.SMEM((8 * cd.shape[0],), jnp.int32),
            pltpu.SMEM((8,), jnp.int32),
        ],
        compiler_params=params(12),
        cost_estimate=cost(12.0),
        name="select_amplitudes",
    )(ab, cd, labels, rank, t, *after)


def product_kernel(blocks, nx, ny, where, ab, t, *rest):
    arrays, (keep, send, largest, acc) = rest[:-4], rest[-4:]
    x, y, core = where[0] // ny, where[0] % ny, where[2]
    part = acc.shape[0] // 4
    most = jnp.zeros((8, acc.shape[1]), jnp.float32)
    for b, block in enumerate(blocks):
        v = ((x + nx - b // 2) % nx) * ny + (y + b) % ny
        f = first_of(ab, v)
        first = 0
        for n, column, width in block:
            last = first + width
            p = jnp.dot(
                arrays[n][:, column : column + width],
                t[f, first:last, :],
                preferred_element_type=jnp.float32,
            )
            acc[...] = p if first == 0 else acc[...] + p
            first = last
        most = jnp.maximum(most, jnp.max(jnp.abs(acc[...]).reshape(-1, 8, acc.shape[1]), axis=0))
        for half in range(2):
            for out, c in ((keep, core), (send, 1 - core)):
                row = pl.multiple_of((2 * half + c) * part, part)
                out[v, half] = acc[pl.ds(row, part), :]
    largest[...] = jnp.full(largest.shape, jnp.max(most), jnp.float32)


def product(where, ab, t, blocks):
    shape = jax.ShapeDtypeStruct((t.shape[0], 2, TILE // 4, t.shape[2]), jnp.float32)
    arrays, places = [], []
    for block in blocks:
        places.append([])
        for v, column, width in block:
            if not any(v is a for a in arrays):
                arrays.append(v)
            places[-1].append(([v is a for a in arrays].index(True), column, width))
    return pl.pallas_call(
        functools.partial(product_kernel, places, lax.axis_size("x"), lax.axis_size("yl")),
        out_shape=[shape, shape, jax.ShapeDtypeStruct((8, TILE), jnp.float32)],
        in_specs=[SMEM] * 2 + [VMEM] * (1 + len(arrays)),
        out_specs=[VMEM, VMEM, VMEM],
        scratch_shapes=[pltpu.VMEM((TILE, t.shape[2]), jnp.float32)],
        compiler_params=params(12),
        cost_estimate=cost(1.6),
        name="product",
    )(where, ab, t, *arrays)


def combine_kernel(keep, got, a, b, out):
    top = (a[...] + b[...])[0:1, :]
    up, down = jnp.ones_like(top), jnp.ones_like(top)
    for bits in (64, 32, 8, 4, 2, 1):
        fits = top * (up * 2.0**bits) <= 2.0**15
        up = jnp.where(fits, up * 2.0**bits, up)
        down = jnp.where(fits, down * 2.0**-bits, down)
    lane = lax.broadcasted_iota(jnp.int32, top.shape, 1)
    parts = jnp.zeros_like(top)
    for i in range(SCALES):
        parts = jnp.where(lane == TILE - SCALES + i, jnp.maximum(down, 1.0 / STEP), parts)
        down = jnp.where(down < 1.0 / STEP, down * STEP, 1.0)
    up = jnp.concatenate([up, jnp.where(lane < TILE - SCALES, up, 0.0)], axis=1)
    parts = jnp.concatenate([jnp.zeros_like(top), parts], axis=1)
    for v in range(keep.shape[0]):
        for y in range(keep.shape[1]):
            out[v * keep.shape[1] + y] = (keep[v, y] + got[v, y]) * up + parts


def combine(keep, got, a, b):
    return pl.pallas_call(
        combine_kernel,
        out_shape=jax.ShapeDtypeStruct((keep.shape[0] * keep.shape[1],) + keep.shape[2:], jnp.float32),
        in_specs=[VMEM] * 4,
        out_specs=VMEM,
        compiler_params=params(6),
        cost_estimate=cost(1.2),
        name="combine",
    )(keep, got, a, b)


def spread_kernel(where, ab, labels, rank, spots, parts, own, send):
    total = jnp.zeros(parts.shape[1:], jnp.float32)
    for z in range(parts.shape[0]):
        part = parts[z]
        down = part[0:1, ROWS - SCALES : ROWS - SCALES + 1]
        for i in range(1, SCALES):
            down *= part[0:1, ROWS - SCALES + i : ROWS - SCALES + i + 1]
        total += part * down
    high = total.astype(jnp.bfloat16)
    rest = total - high.astype(jnp.float32)
    middle = rest.astype(jnp.bfloat16)
    low = (rest - middle.astype(jnp.float32)).astype(jnp.bfloat16)
    split = jnp.concatenate([high, middle, low], axis=0)
    n = total.shape[0]

    def placed(spot):
        x = jnp.dot(split, one_hot((total.shape[1], spot.shape[1]), spot), preferred_element_type=jnp.float32)
        return x[:n] + (x[n : 2 * n] + x[2 * n :])

    for o in range(0, send.shape[0], 2):
        x = placed(spots[:, o * TILE : (o + 2) * TILE])
        send[o] = x[:, :TILE]
        send[o + 1] = x[:, TILE:]
    mine = ab[where[1]]
    for k in range(0, own.shape[1], 2 * TILE):
        span = slice(k, k + 2 * TILE)
        own[:, span] = placed(jnp.where(labels[:, span] == mine, rank[:, span], -1))


def spread(where, ab, labels, rank, spots, parts):
    return pl.pallas_call(
        spread_kernel,
        out_shape=[
            jax.ShapeDtypeStruct((parts.shape[1], labels.shape[1]), jnp.float32),
            jax.ShapeDtypeStruct((spots.shape[1] // TILE, parts.shape[1], TILE), jnp.float32),
        ],
        in_specs=[SMEM, SMEM] + [VMEM] * 4,
        out_specs=[VMEM, VMEM],
        compiler_params=params(6),
        cost_estimate=cost(1.7),
        name="spread",
    )(where, ab, labels, rank, spots, parts)


def finish_kernel(own, got, out, turned):
    local, orbitals, width = turned.shape
    for o in range(got.shape[0]):
        x = jnp.transpose(got[o])
        for i in range(local):
            turned[i, o * local : (o + 1) * local, :] = x[i * local : (i + 1) * local, :]
    for i in range(local):
        mine = own[:, i * orbitals : (i + 1) * orbitals]
        out[i * width : (i + 1) * width, :] = (2.0 * mine - jnp.transpose(turned[i])).astype(jnp.bfloat16)


def finish(own, got, local, orbitals):
    width = own.shape[0]
    return pl.pallas_call(
        finish_kernel,
        out_shape=jax.ShapeDtypeStruct((local * width, orbitals), jnp.bfloat16),
        in_specs=[VMEM, VMEM],
        out_specs=VMEM,
        scratch_shapes=[pltpu.VMEM((local, orbitals, width), jnp.float32)],
        compiler_params=params(4),
        cost_estimate=cost(0.4),
        name="finish",
    )(own, got)


def join_kernel(after, *refs):
    ins, out = refs[after:-1], refs[-1]
    first = 0
    for v in ins:
        out[:, first : first + v.shape[1]] = v[...]
        first += v.shape[1]


def join(blocks, after):
    return pl.pallas_call(
        functools.partial(join_kernel, len(after)),
        out_shape=jax.ShapeDtypeStruct(
            (blocks[0].shape[0], sum(v.shape[1] for v in blocks)), blocks[0].dtype
        ),
        in_specs=[ANY] * len(after) + [VMEM] * len(blocks),
        out_specs=VMEM,
        compiler_params=params(6),
        cost_estimate=cost(0.4),
        name="join",
    )(*after, *blocks)


def gather(pieces):
    nx, ny = lax.axis_size("x"), lax.axis_size("yl")
    swap = shifted("yl", ny, 1)
    up, down = shifted("x", nx, 1), shifted("x", nx, nx - 1)
    first, rest = pieces[0], pieces[1:]
    width = first.shape[1]
    partner = swap(first)
    early = [[shifted("x", nx, step)(v) for v in rest] for step in range(1, nx)]
    mine = {1: up(first), nx - 1: down(first)}
    other = {1: up(partner), nx - 1: down(partner)}
    for step in range(2, nx - 1):
        mine[step] = up(mine[step - 1])
        other[nx - step] = down(other[nx - step + 1])
    blocks = [[(first, 0, width)], [(partner, 0, width)]]
    for step in range(1, nx):
        blocks += [[(mine[step], 0, width)], [(other[step], 0, width)]]
    passed = []
    if rest:
        through = [rest[0]] + [v[0] for v in early]
        passed = [join(through, [partner])]
        back = swap(passed[0])
        step = rest[0].shape[1]
        for k, v in enumerate(through):
            blocks[2 * k].append((v, 0, step))
            blocks[2 * k + 1].append((back, k * step, step))
    return blocks, passed


def dense(amplitudes, integrals, occ_irrep, ab_irrep, cd_irrep):
    rows, cols = amplitudes.shape
    orbitals = occ_irrep.shape[0]
    groups = lax.axis_size("x") * lax.axis_size("yl")
    local = orbitals // groups
    me = lax.axis_index("x") * lax.axis_size("yl") + lax.axis_index("yl")
    blocks = lax.all_to_all(
        jnp.broadcast_to(integrals, (groups,) + integrals.shape), ("x", "yl"), 0, 0, tiled=True
    )
    mine = lax.dynamic_slice_in_dim(occ_irrep, me * local, local)
    pair = jnp.bitwise_xor(mine[:, None], occ_irrep[None, :]).reshape(rows)
    col = jnp.repeat(cd_irrep, TILE)
    masked_t = jnp.where(pair[:, None] == col[None, :], amplitudes, 0)
    masked_v = jnp.where(ab_irrep[:, None, None] == col[None, None, :], blocks, 0)
    part = lax.dot_general(
        masked_v.reshape(-1, cols), masked_t, (((1,), (1,)), ((), ())), preferred_element_type=jnp.float32
    )
    part = part.reshape(groups * 4, TILE // 4, rows)
    part = lax.all_to_all(part, ("vir", "yh", "core"), 0, 0, tiled=True).sum(0)
    own = part.reshape(TILE // 4, local, groups, local).transpose(2, 0, 1, 3)
    got = lax.all_to_all(own, ("x", "yl"), 0, 0, tiled=True)
    out = 2.0 * own.transpose(2, 0, 3, 1) - got.transpose(3, 0, 2, 1)
    return out.reshape(local, orbitals, TILE // 4).astype(jnp.bfloat16)


def per_device(amplitudes, integrals, occ_irrep, ab_irrep, cd_irrep):
    groups = lax.axis_size("x") * lax.axis_size("yl")
    orbitals = occ_irrep.shape[0]
    rows = amplitudes.shape[0]
    me = lax.axis_index("x") * lax.axis_size("yl") + lax.axis_index("yl")
    where = jnp.stack([me, lax.axis_index("vir"), lax.axis_index("core")]).astype(jnp.int32)
    tiles = cd_irrep.shape[0]

    def partial_sums(skip, slots, found, blocks, passed):
        selected = select(skip, slots, ab_irrep, cd_irrep, *found[:2], amplitudes, passed)
        return product(where, ab_irrep, selected, blocks)

    done = sum(FIRST)
    more, *packed = pack(0, FIRST, where, ab_irrep, cd_irrep, integrals)
    blocks, passed = gather(packed)
    found = ranks(where, occ_irrep, ab_irrep, rows, groups, [])
    sums = partial_sums(0, done, found, blocks, passed)

    def rest(sums, v, found):
        _, packed = pack(done, (tiles - done,), where, ab_irrep, cd_irrep, v)
        blocks, _ = gather([packed])
        return jax.tree.map(jnp.add, list(sums), list(partial_sums(done, tiles - done, found, blocks, [])))

    keep, send, largest = lax.cond(
        more[0] > 0, rest, lambda sums, v, found: list(sums), list(sums), integrals, found
    )
    labels, rank, spots, over = found
    other = shifted("core", 2, 1)
    part = combine(keep, other(send), largest, other(largest)).astype(jnp.float16)
    part = lax.all_to_all(part, ("vir", "yh"), 0, 0, tiled=True).astype(jnp.float32)
    own, send = spread(where, ab_irrep, labels, rank, spots, part)
    got = lax.all_to_all(send, ("x", "yl"), 0, 0, tiled=True)
    out = lax.cond(
        over[0] > 0,
        lambda own, got, *a: jnp.swapaxes(dense(*a), 1, 2).reshape(-1, orbitals),
        lambda own, got, *a: finish(own, got, rows // orbitals, orbitals),
        *(own, got, amplitudes, integrals, occ_irrep, ab_irrep, cd_irrep),
    )
    return jnp.swapaxes(out.reshape(rows // orbitals, -1, orbitals), 1, 2)


def solution(mesh):
    occ, vir, con = (mesh.shape[a] for a in ("occ", "vir", "con"))
    split = Mesh(
        mesh.devices.reshape(occ // 2, 2, vir, 2, con // 2), ("x", "yl", "vir", "yh", "core")
    )
    cd = ("vir", "yh", "core")
    return jax.shard_map(
        per_device,
        mesh=split,
        in_specs=(P(("x", "yl"), cd), P(("x", "yl"), cd), P(), P(), P(cd)),
        out_specs=P(("x", "yl"), None, cd),
        check_vma=False,
    )
```

```python
import functools

import jax
import jax.numpy as jnp
from jax import lax
from jax.experimental import pallas as pl
from jax.experimental.pallas import tpu as pltpu
from jax.sharding import Mesh, PartitionSpec as P

TILE = 128
ROWS = 256
SCALES = 8
STEP = 2.0**14
FIRST = (7, 4)
MIB = 1 << 20
SMEM = pl.BlockSpec(memory_space=pltpu.SMEM)
VMEM = pl.BlockSpec(memory_space=pltpu.VMEM)
ANY = pl.BlockSpec(memory_space=pl.ANY)


def shifted(axis, size, step):
    return lambda a: lax.ppermute(a, axis, [(i, (i + step) % size) for i in range(size)])


def cost(us):
    return pl.CostEstimate(flops=int(us * 1.1e9), bytes_accessed=0, transcendentals=0)


def params(mib):
    return pltpu.CompilerParams(vmem_limit_bytes=mib * MIB)


def pack_kernel(skip, where, ab, cd, v, more, *rest):
    outs, count = rest[:-1], rest[-1]
    mine = ab[where[0]]
    for c in range(count.shape[0]):
        count[c] = 0

    @pl.loop(0, cd.shape[0])
    def _(t):
        label = cd[t]
        slot = count[label] - skip
        count[label] = count[label] + 1

        @pl.when(label == mine)
        def _():
            tile = v[:, pl.ds(pl.multiple_of(t * TILE, TILE), TILE)]
            first = 0
            for out in outs:
                place = slot - first
                slots = out.shape[1] // TILE

                @pl.when((place >= 0) & (place < slots))
                def _():
                    out[:, pl.ds(pl.multiple_of(place * TILE, TILE), TILE)] = tile

                first += slots

    first = skip
    for out in outs:
        slots = out.shape[1] // TILE

        @pl.loop(jnp.clip(count[mine] - first, 0, slots), slots)
        def _(slot):
            out[:, pl.ds(pl.multiple_of(slot * TILE, TILE), TILE)] = jnp.zeros((v.shape[0], TILE), v.dtype)

        first += slots
    most = count[ab[0]]
    for a in range(1, ab.shape[0]):
        most = jnp.maximum(most, count[ab[a]])
    more[0] = (most > first).astype(jnp.int32)


def pack(skip, pieces, where, ab, cd, v):
    return pl.pallas_call(
        functools.partial(pack_kernel, skip),
        out_shape=[jax.ShapeDtypeStruct((1,), jnp.int32)]
        + [jax.ShapeDtypeStruct((v.shape[0], slots * TILE), v.dtype) for slots in pieces],
        in_specs=[SMEM, SMEM, SMEM, VMEM],
        out_specs=[SMEM] + [VMEM] * len(pieces),
        scratch_shapes=[pltpu.SMEM((8,), jnp.int32)],
        compiler_params=params(4),
        cost_estimate=cost(2.0),
        name="pack_integrals",
    )(where, ab, cd, v)


def one_hot(shape, spot):
    match = lax.broadcasted_iota(jnp.int32, shape, 0) == spot
    return match.astype(jnp.float32).astype(jnp.bfloat16)


def rank_kernel(after, where, occ, ab, occ_row, *rest):
    labels, rank, spots, over = rest[after:]
    orbitals, rows = occ_row.shape[1], labels.shape[1]
    local = rows // orbitals
    irreps, abt = 8, ab.shape[0]
    me, mine = where[0], ab[where[1]]
    for i in range(local):
        labels[:, i * orbitals : (i + 1) * orbitals] = occ_row[...] ^ occ[me * local + i]

    label = labels[...]
    is_label = lax.broadcasted_iota(jnp.int32, (irreps, rows), 0) == label
    marks = is_label.astype(jnp.float32).astype(jnp.bfloat16)

    @pl.loop(0, rows // TILE)
    def _(k):
        first = pl.multiple_of(k * TILE, TILE)
        shape = (rows, TILE)
        before = lax.broadcasted_iota(jnp.int32, shape, 0) < first + lax.broadcasted_iota(
            jnp.int32, shape, 1
        )
        ahead = jnp.dot(
            marks, before.astype(jnp.float32).astype(jnp.bfloat16), preferred_element_type=jnp.float32
        )
        own = lax.broadcasted_iota(jnp.int32, (irreps, TILE), 0) == labels[:, pl.ds(first, TILE)]
        rank[:, pl.ds(first, TILE)] = jnp.sum(
            jnp.where(own, ahead, 0.0), axis=0, keepdims=True
        ).astype(jnp.int32)

    column = lax.broadcasted_iota(jnp.int32, (abt, orbitals), 0)
    partner = occ_row[...]
    want = jnp.zeros((abt, orbitals), jnp.int32)
    for v in range(abt):
        want = jnp.where(column == v, ab[v], want)
    want = want ^ partner
    of_irrep = lax.broadcasted_iota(jnp.int32, (irreps, orbitals), 0) == partner
    count = jnp.sum(of_irrep.astype(jnp.float32), axis=1, keepdims=True)
    met = jnp.zeros((abt, orbitals), jnp.float32)
    for c in range(irreps):
        met = jnp.where(want == c, count[c : c + 1, :], met)
    shape = (orbitals, TILE)
    group = lax.broadcasted_iota(jnp.int32, shape, 0) // local == lax.broadcasted_iota(jnp.int32, shape, 1)
    held = jnp.dot(
        met.astype(jnp.bfloat16),
        group.astype(jnp.float32).astype(jnp.bfloat16),
        preferred_element_type=jnp.float32,
    )
    over[0] = (jnp.max(held) > ROWS - SCALES).astype(jnp.int32)

    which = lax.broadcasted_iota(jnp.int32, (8, rows), 0)
    place = rank[...]
    values = jnp.where(
        which == 0, label, jnp.where(which == 1, place % 256, jnp.where(which == 2, place // 256, 0))
    )
    values = values.astype(jnp.float32).astype(jnp.bfloat16)

    @pl.loop(0, spots.shape[1] // TILE)
    def _(owner):
        lane = lax.broadcasted_iota(jnp.int32, (1, TILE), 1)
        j, i = lane // local, lane % local
        source = jnp.where(j < local, i * orbitals + owner * local + j, -1)
        moved = jnp.dot(
            values, one_hot((rows, TILE), source), preferred_element_type=jnp.float32
        ).astype(jnp.int32)
        here = (moved[0:1] == mine) & (j < local)
        spots[:, pl.ds(pl.multiple_of(owner * TILE, TILE), TILE)] = jnp.where(
            here, moved[1:2] + 256 * moved[2:3], -1
        )


def ranks(where, occ, ab, rows, groups, after):
    return pl.pallas_call(
        functools.partial(rank_kernel, len(after)),
        out_shape=[
            jax.ShapeDtypeStruct((1, rows), jnp.int32),
            jax.ShapeDtypeStruct((1, rows), jnp.int32),
            jax.ShapeDtypeStruct((1, groups * TILE), jnp.int32),
            jax.ShapeDtypeStruct((1,), jnp.int32),
        ],
        in_specs=[SMEM, SMEM, SMEM, VMEM] + [ANY] * len(after),
        out_specs=[VMEM, VMEM, VMEM, SMEM],
        compiler_params=params(4),
        cost_estimate=cost(3.3),
        name="ranks",
    )(where, occ, ab, occ.reshape(1, -1), *after)


def select_kernel(skip, after, ab, cd, labels, rank, t, *rest):
    out, hot, tile_of, count = rest[after:]
    tiles, slots = cd.shape[0], out.shape[1] // TILE
    for c in range(count.shape[0]):
        count[c] = 0

    @pl.loop(0, tiles)
    def _(i):
        label = cd[i]
        tile_of[label * tiles + count[label]] = i
        count[label] = count[label] + 1

    @pl.loop(0, ab.shape[0])
    def _(v):
        want = ab[v]

        @pl.when(first_of(ab, v) == v)
        def _():
            hot[...] = one_hot(hot.shape, jnp.where(labels[...] == want, rank[...], -1))
            used = jnp.clip(count[want] - skip, 0, slots)

            @pl.loop(0, (used + 1) // 2)
            def _(s):
                spans = []
                for k in range(2):
                    i = tile_of[jnp.minimum(want * tiles + skip + 2 * s + k, want * tiles + skip + used - 1)]
                    spans.append(t[:, pl.ds(pl.multiple_of(i * TILE, TILE), TILE)])
                rows_in = jnp.dot(hot[...], jnp.concatenate(spans, axis=1), preferred_element_type=jnp.float32)
                out[v, pl.ds(pl.multiple_of(s * 2 * TILE, 2 * TILE), 2 * TILE), :] = jnp.transpose(
                    rows_in
                ).astype(jnp.bfloat16)

            @pl.loop(2 * ((used + 1) // 2), slots)
            def _(s):
                out[v, pl.ds(pl.multiple_of(s * TILE, TILE), TILE), :] = jnp.zeros(
                    (TILE, out.shape[2]), jnp.bfloat16
                )


def first_of(ab, v):
    want = ab[v]
    first = jnp.int32(0)
    for a in reversed(range(ab.shape[0])):
        first = jnp.where(ab[a] == want, a, first)
    return first


def select(skip, slots, ab, cd, labels, rank, t, after):
    return pl.pallas_call(
        functools.partial(select_kernel, skip, len(after)),
        out_shape=jax.ShapeDtypeStruct((ab.shape[0], slots * TILE, ROWS), t.dtype),
        in_specs=[SMEM, SMEM, VMEM, VMEM, VMEM] + [ANY] * len(after),
        out_specs=VMEM,
        scratch_shapes=[
            pltpu.VMEM((ROWS, t.shape[0]), jnp.bfloat16),
            pltpu.SMEM((8 * cd.shape[0],), jnp.int32),
            pltpu.SMEM((8,), jnp.int32),
        ],
        compiler_params=params(12),
        cost_estimate=cost(12.0),
        name="select_amplitudes",
    )(ab, cd, labels, rank, t, *after)


def product_kernel(blocks, nx, ny, where, ab, t, *rest):
    arrays, (keep, send, largest, acc) = rest[:-4], rest[-4:]
    x, y, core = where[0] // ny, where[0] % ny, where[2]
    part = acc.shape[0] // 4
    most = jnp.zeros((8, acc.shape[1]), jnp.float32)
    for b, block in enumerate(blocks):
        v = ((x + nx - b // 2) % nx) * ny + (y + b) % ny
        f = first_of(ab, v)
        first = 0
        for n, column, width in block:
            last = first + width
            p = jnp.dot(
                arrays[n][:, column : column + width],
                t[f, first:last, :],
                preferred_element_type=jnp.float32,
            )
            acc[...] = p if first == 0 else acc[...] + p
            first = last
        most = jnp.maximum(most, jnp.max(jnp.abs(acc[...]).reshape(-1, 8, acc.shape[1]), axis=0))
        for half in range(2):
            for out, c in ((keep, core), (send, 1 - core)):
                row = pl.multiple_of((2 * half + c) * part, part)
                out[v, half] = acc[pl.ds(row, part), :]
    largest[...] = jnp.full(largest.shape, jnp.max(most), jnp.float32)


def product(where, ab, t, blocks):
    shape = jax.ShapeDtypeStruct((t.shape[0], 2, TILE // 4, t.shape[2]), jnp.float32)
    arrays, places = [], []
    for block in blocks:
        places.append([])
        for v, column, width in block:
            if not any(v is a for a in arrays):
                arrays.append(v)
            places[-1].append(([v is a for a in arrays].index(True), column, width))
    return pl.pallas_call(
        functools.partial(product_kernel, places, lax.axis_size("x"), lax.axis_size("yl")),
        out_shape=[shape, shape, jax.ShapeDtypeStruct((8, TILE), jnp.float32)],
        in_specs=[SMEM] * 2 + [VMEM] * (1 + len(arrays)),
        out_specs=[VMEM, VMEM, VMEM],
        scratch_shapes=[pltpu.VMEM((TILE, t.shape[2]), jnp.float32)],
        compiler_params=params(12),
        cost_estimate=cost(1.6),
        name="product",
    )(where, ab, t, *arrays)


def combine_kernel(keep, got, a, b, out):
    top = (a[...] + b[...])[0:1, :]
    up, down = jnp.ones_like(top), jnp.ones_like(top)
    for bits in (64, 32, 8, 4, 2, 1):
        fits = top * (up * 2.0**bits) <= 2.0**15
        up = jnp.where(fits, up * 2.0**bits, up)
        down = jnp.where(fits, down * 2.0**-bits, down)
    lane = lax.broadcasted_iota(jnp.int32, top.shape, 1)
    parts = jnp.zeros_like(top)
    for i in range(SCALES):
        parts = jnp.where(lane == TILE - SCALES + i, jnp.maximum(down, 1.0 / STEP), parts)
        down = jnp.where(down < 1.0 / STEP, down * STEP, 1.0)
    up = jnp.concatenate([up, jnp.where(lane < TILE - SCALES, up, 0.0)], axis=1)
    parts = jnp.concatenate([jnp.zeros_like(top), parts], axis=1)
    for v in range(keep.shape[0]):
        for y in range(keep.shape[1]):
            out[v * keep.shape[1] + y] = (keep[v, y] + got[v, y]) * up + parts


def combine(keep, got, a, b):
    return pl.pallas_call(
        combine_kernel,
        out_shape=jax.ShapeDtypeStruct((keep.shape[0] * keep.shape[1],) + keep.shape[2:], jnp.float32),
        in_specs=[VMEM] * 4,
        out_specs=VMEM,
        compiler_params=params(6),
        cost_estimate=cost(1.2),
        name="combine",
    )(keep, got, a, b)


def spread_kernel(where, ab, labels, rank, spots, parts, own, send):
    total = jnp.zeros(parts.shape[1:], jnp.float32)
    for z in range(parts.shape[0]):
        part = parts[z]
        down = part[0:1, ROWS - SCALES : ROWS - SCALES + 1]
        for i in range(1, SCALES):
            down *= part[0:1, ROWS - SCALES + i : ROWS - SCALES + i + 1]
        total += part * down
    high = total.astype(jnp.bfloat16)
    rest = total - high.astype(jnp.float32)
    middle = rest.astype(jnp.bfloat16)
    low = (rest - middle.astype(jnp.float32)).astype(jnp.bfloat16)
    split = jnp.concatenate([high, middle, low], axis=0)
    n = total.shape[0]

    def placed(spot):
        x = jnp.dot(split, one_hot((total.shape[1], spot.shape[1]), spot), preferred_element_type=jnp.float32)
        return x[:n] + (x[n : 2 * n] + x[2 * n :])

    for o in range(0, send.shape[0], 2):
        x = placed(spots[:, o * TILE : (o + 2) * TILE])
        send[o] = x[:, :TILE]
        send[o + 1] = x[:, TILE:]
    mine = ab[where[1]]
    for k in range(0, own.shape[1], 2 * TILE):
        span = slice(k, k + 2 * TILE)
        own[:, span] = placed(jnp.where(labels[:, span] == mine, rank[:, span], -1))


def spread(where, ab, labels, rank, spots, parts):
    return pl.pallas_call(
        spread_kernel,
        out_shape=[
            jax.ShapeDtypeStruct((parts.shape[1], labels.shape[1]), jnp.float32),
            jax.ShapeDtypeStruct((spots.shape[1] // TILE, parts.shape[1], TILE), jnp.float32),
        ],
        in_specs=[SMEM, SMEM] + [VMEM] * 4,
        out_specs=[VMEM, VMEM],
        compiler_params=params(6),
        cost_estimate=cost(1.7),
        name="spread",
    )(where, ab, labels, rank, spots, parts)


def finish_kernel(own, got, out, turned):
    local, orbitals, width = turned.shape
    for o in range(got.shape[0]):
        x = jnp.transpose(got[o])
        for i in range(local):
            turned[i, o * local : (o + 1) * local, :] = x[i * local : (i + 1) * local, :]
    for i in range(local):
        mine = own[:, i * orbitals : (i + 1) * orbitals]
        out[i * width : (i + 1) * width, :] = (2.0 * mine - jnp.transpose(turned[i])).astype(jnp.bfloat16)


def finish(own, got, local, orbitals):
    width = own.shape[0]
    return pl.pallas_call(
        finish_kernel,
        out_shape=jax.ShapeDtypeStruct((local * width, orbitals), jnp.bfloat16),
        in_specs=[VMEM, VMEM],
        out_specs=VMEM,
        scratch_shapes=[pltpu.VMEM((local, orbitals, width), jnp.float32)],
        compiler_params=params(4),
        cost_estimate=cost(0.4),
        name="finish",
    )(own, got)


def join_kernel(after, *refs):
    ins, out = refs[after:-1], refs[-1]
    first = 0
    for v in ins:
        out[:, first : first + v.shape[1]] = v[...]
        first += v.shape[1]


def join(blocks, after):
    return pl.pallas_call(
        functools.partial(join_kernel, len(after)),
        out_shape=jax.ShapeDtypeStruct(
            (blocks[0].shape[0], sum(v.shape[1] for v in blocks)), blocks[0].dtype
        ),
        in_specs=[ANY] * len(after) + [VMEM] * len(blocks),
        out_specs=VMEM,
        compiler_params=params(6),
        cost_estimate=cost(0.4),
        name="join",
    )(*after, *blocks)


def gather(pieces):
    nx, ny = lax.axis_size("x"), lax.axis_size("yl")
    swap = shifted("yl", ny, 1)
    up, down = shifted("x", nx, 1), shifted("x", nx, nx - 1)
    first, rest = pieces[0], pieces[1:]
    width = first.shape[1]
    partner = swap(first)
    early = [[shifted("x", nx, step)(v) for v in rest] for step in range(1, nx)]
    mine = {1: up(first), nx - 1: down(first)}
    other = {1: up(partner), nx - 1: down(partner)}
    for step in range(2, nx - 1):
        mine[step] = up(mine[step - 1])
        other[nx - step] = down(other[nx - step + 1])
    blocks = [[(first, 0, width)], [(partner, 0, width)]]
    for step in range(1, nx):
        blocks += [[(mine[step], 0, width)], [(other[step], 0, width)]]
    passed = []
    if rest:
        through = [rest[0]] + [v[0] for v in early]
        passed = [join(through, [partner])]
        back = swap(passed[0])
        step = rest[0].shape[1]
        for k, v in enumerate(through):
            blocks[2 * k].append((v, 0, step))
            blocks[2 * k + 1].append((back, k * step, step))
    return blocks, passed


def dense(amplitudes, integrals, occ_irrep, ab_irrep, cd_irrep):
    rows, cols = amplitudes.shape
    orbitals = occ_irrep.shape[0]
    groups = lax.axis_size("x") * lax.axis_size("yl")
    local = orbitals // groups
    me = lax.axis_index("x") * lax.axis_size("yl") + lax.axis_index("yl")
    blocks = lax.all_to_all(
        jnp.broadcast_to(integrals, (groups,) + integrals.shape), ("x", "yl"), 0, 0, tiled=True
    )
    mine = lax.dynamic_slice_in_dim(occ_irrep, me * local, local)
    pair = jnp.bitwise_xor(mine[:, None], occ_irrep[None, :]).reshape(rows)
    col = jnp.repeat(cd_irrep, TILE)
    masked_t = jnp.where(pair[:, None] == col[None, :], amplitudes, 0)
    masked_v = jnp.where(ab_irrep[:, None, None] == col[None, None, :], blocks, 0)
    part = lax.dot_general(
        masked_v.reshape(-1, cols), masked_t, (((1,), (1,)), ((), ())), preferred_element_type=jnp.float32
    )
    part = part.reshape(groups * 4, TILE // 4, rows)
    part = lax.all_to_all(part, ("vir", "yh", "core"), 0, 0, tiled=True).sum(0)
    own = part.reshape(TILE // 4, local, groups, local).transpose(2, 0, 1, 3)
    got = lax.all_to_all(own, ("x", "yl"), 0, 0, tiled=True)
    out = 2.0 * own.transpose(2, 0, 3, 1) - got.transpose(3, 0, 2, 1)
    return out.reshape(local, orbitals, TILE // 4).astype(jnp.bfloat16)


def per_device(amplitudes, integrals, occ_irrep, ab_irrep, cd_irrep):
    groups = lax.axis_size("x") * lax.axis_size("yl")
    orbitals = occ_irrep.shape[0]
    rows = amplitudes.shape[0]
    me = lax.axis_index("x") * lax.axis_size("yl") + lax.axis_index("yl")
    where = jnp.stack([me, lax.axis_index("vir"), lax.axis_index("core")]).astype(jnp.int32)
    tiles = cd_irrep.shape[0]

    def partial_sums(skip, slots, found, blocks, passed):
        selected = select(skip, slots, ab_irrep, cd_irrep, *found[:2], amplitudes, passed)
        return product(where, ab_irrep, selected, blocks)

    done = sum(FIRST)
    more, *packed = pack(0, FIRST, where, ab_irrep, cd_irrep, integrals)
    blocks, passed = gather(packed)
    found = ranks(where, occ_irrep, ab_irrep, rows, groups, [])
    sums = partial_sums(0, done, found, blocks, passed)

    def rest(sums, v, found):
        _, packed = pack(done, (tiles - done,), where, ab_irrep, cd_irrep, v)
        blocks, _ = gather([packed])
        return jax.tree.map(jnp.add, list(sums), list(partial_sums(done, tiles - done, found, blocks, [])))

    keep, send, largest = lax.cond(
        more[0] > 0, rest, lambda sums, v, found: list(sums), list(sums), integrals, found
    )
    labels, rank, spots, over = found
    other = shifted("core", 2, 1)
    part = combine(keep, other(send), largest, other(largest)).astype(jnp.float16)
    part = lax.all_to_all(part, ("vir", "yh"), 0, 0, tiled=True).astype(jnp.float32)
    own, send = spread(where, ab_irrep, labels, rank, spots, part)
    got = lax.all_to_all(send, ("x", "yl"), 0, 0, tiled=True)
    out = lax.cond(
        over[0] > 0,
        lambda own, got, *a: jnp.swapaxes(dense(*a), 1, 2).reshape(-1, orbitals),
        lambda own, got, *a: finish(own, got, rows // orbitals, orbitals),
        *(own, got, amplitudes, integrals, occ_irrep, ab_irrep, cd_irrep),
    )
    return jnp.swapaxes(out.reshape(rows // orbitals, -1, orbitals), 1, 2)


def solution(mesh):
    occ, vir, con = (mesh.shape[a] for a in ("occ", "vir", "con"))
    split = Mesh(
        mesh.devices.reshape(occ // 2, 2, vir, 2, con // 2), ("x", "yl", "vir", "yh", "core")
    )
    cd = ("vir", "yh", "core")
    return jax.shard_map(
        per_device,
        mesh=split,
        in_specs=(P(("x", "yl"), cd), P(("x", "yl"), cd), P(), P(), P(cd)),
        out_specs=P(("x", "yl"), None, cd),
        check_vma=False,
    )
```

```python
import functools

import jax
import jax.numpy as jnp
from jax import lax
from jax.experimental import pallas as pl
from jax.experimental.pallas import tpu as pltpu
from jax.sharding import Mesh, PartitionSpec as P

TILE = 128
ROWS = 256
SCALES = 8
STEP = 2.0**14
FIRST = (7, 4)
MIB = 1 << 20
SMEM = pl.BlockSpec(memory_space=pltpu.SMEM)
VMEM = pl.BlockSpec(memory_space=pltpu.VMEM)
ANY = pl.BlockSpec(memory_space=pl.ANY)


def shifted(axis, size, step):
    return lambda a: lax.ppermute(a, axis, [(i, (i + step) % size) for i in range(size)])


def cost(us):
    return pl.CostEstimate(flops=int(us * 1.1e9), bytes_accessed=0, transcendentals=0)


def params(mib):
    return pltpu.CompilerParams(vmem_limit_bytes=mib * MIB)


def pack_kernel(skip, where, ab, cd, v, more, *rest):
    outs, count = rest[:-1], rest[-1]
    mine = ab[where[0]]
    for c in range(count.shape[0]):
        count[c] = 0

    @pl.loop(0, cd.shape[0])
    def _(t):
        label = cd[t]
        slot = count[label] - skip
        count[label] = count[label] + 1

        @pl.when(label == mine)
        def _():
            tile = v[:, pl.ds(pl.multiple_of(t * TILE, TILE), TILE)]
            first = 0
            for out in outs:
                place = slot - first
                slots = out.shape[1] // TILE

                @pl.when((place >= 0) & (place < slots))
                def _():
                    out[:, pl.ds(pl.multiple_of(place * TILE, TILE), TILE)] = tile

                first += slots

    first = skip
    for out in outs:
        slots = out.shape[1] // TILE

        @pl.loop(jnp.clip(count[mine] - first, 0, slots), slots)
        def _(slot):
            out[:, pl.ds(pl.multiple_of(slot * TILE, TILE), TILE)] = jnp.zeros((v.shape[0], TILE), v.dtype)

        first += slots
    most = count[ab[0]]
    for a in range(1, ab.shape[0]):
        most = jnp.maximum(most, count[ab[a]])
    more[0] = (most > first).astype(jnp.int32)


def pack(skip, pieces, where, ab, cd, v):
    return pl.pallas_call(
        functools.partial(pack_kernel, skip),
        out_shape=[jax.ShapeDtypeStruct((1,), jnp.int32)]
        + [jax.ShapeDtypeStruct((v.shape[0], slots * TILE), v.dtype) for slots in pieces],
        in_specs=[SMEM, SMEM, SMEM, VMEM],
        out_specs=[SMEM] + [VMEM] * len(pieces),
        scratch_shapes=[pltpu.SMEM((8,), jnp.int32)],
        compiler_params=params(4),
        cost_estimate=cost(2.0),
        name="pack_integrals",
    )(where, ab, cd, v)


def one_hot(shape, spot):
    match = lax.broadcasted_iota(jnp.int32, shape, 0) == spot
    return match.astype(jnp.float32).astype(jnp.bfloat16)


def rank_kernel(after, where, occ, ab, occ_row, *rest):
    labels, rank, spots, over = rest[after:]
    orbitals, rows = occ_row.shape[1], labels.shape[1]
    local = rows // orbitals
    irreps, abt = 8, ab.shape[0]
    me, mine = where[0], ab[where[1]]
    for i in range(local):
        labels[:, i * orbitals : (i + 1) * orbitals] = occ_row[...] ^ occ[me * local + i]

    label = labels[...]
    is_label = lax.broadcasted_iota(jnp.int32, (irreps, rows), 0) == label
    marks = is_label.astype(jnp.float32).astype(jnp.bfloat16)

    @pl.loop(0, rows // TILE)
    def _(k):
        first = pl.multiple_of(k * TILE, TILE)
        shape = (rows, TILE)
        before = lax.broadcasted_iota(jnp.int32, shape, 0) < first + lax.broadcasted_iota(
            jnp.int32, shape, 1
        )
        ahead = jnp.dot(
            marks, before.astype(jnp.float32).astype(jnp.bfloat16), preferred_element_type=jnp.float32
        )
        own = lax.broadcasted_iota(jnp.int32, (irreps, TILE), 0) == labels[:, pl.ds(first, TILE)]
        rank[:, pl.ds(first, TILE)] = jnp.sum(
            jnp.where(own, ahead, 0.0), axis=0, keepdims=True
        ).astype(jnp.int32)

    column = lax.broadcasted_iota(jnp.int32, (abt, orbitals), 0)
    partner = occ_row[...]
    want = jnp.zeros((abt, orbitals), jnp.int32)
    for v in range(abt):
        want = jnp.where(column == v, ab[v], want)
    want = want ^ partner
    of_irrep = lax.broadcasted_iota(jnp.int32, (irreps, orbitals), 0) == partner
    count = jnp.sum(of_irrep.astype(jnp.float32), axis=1, keepdims=True)
    met = jnp.zeros((abt, orbitals), jnp.float32)
    for c in range(irreps):
        met = jnp.where(want == c, count[c : c + 1, :], met)
    shape = (orbitals, TILE)
    group = lax.broadcasted_iota(jnp.int32, shape, 0) // local == lax.broadcasted_iota(jnp.int32, shape, 1)
    held = jnp.dot(
        met.astype(jnp.bfloat16),
        group.astype(jnp.float32).astype(jnp.bfloat16),
        preferred_element_type=jnp.float32,
    )
    over[0] = (jnp.max(held) > ROWS - SCALES).astype(jnp.int32)

    which = lax.broadcasted_iota(jnp.int32, (8, rows), 0)
    place = rank[...]
    values = jnp.where(
        which == 0, label, jnp.where(which == 1, place % 256, jnp.where(which == 2, place // 256, 0))
    )
    values = values.astype(jnp.float32).astype(jnp.bfloat16)

    @pl.loop(0, spots.shape[1] // TILE)
    def _(owner):
        lane = lax.broadcasted_iota(jnp.int32, (1, TILE), 1)
        j, i = lane // local, lane % local
        source = jnp.where(j < local, i * orbitals + owner * local + j, -1)
        moved = jnp.dot(
            values, one_hot((rows, TILE), source), preferred_element_type=jnp.float32
        ).astype(jnp.int32)
        here = (moved[0:1] == mine) & (j < local)
        spots[:, pl.ds(pl.multiple_of(owner * TILE, TILE), TILE)] = jnp.where(
            here, moved[1:2] + 256 * moved[2:3], -1
        )


def ranks(where, occ, ab, rows, groups, after):
    return pl.pallas_call(
        functools.partial(rank_kernel, len(after)),
        out_shape=[
            jax.ShapeDtypeStruct((1, rows), jnp.int32),
            jax.ShapeDtypeStruct((1, rows), jnp.int32),
            jax.ShapeDtypeStruct((1, groups * TILE), jnp.int32),
            jax.ShapeDtypeStruct((1,), jnp.int32),
        ],
        in_specs=[SMEM, SMEM, SMEM, VMEM] + [ANY] * len(after),
        out_specs=[VMEM, VMEM, VMEM, SMEM],
        compiler_params=params(4),
        cost_estimate=cost(3.3),
        name="ranks",
    )(where, occ, ab, occ.reshape(1, -1), *after)


def select_kernel(skip, after, ab, cd, labels, rank, t, *rest):
    out, hot, tile_of, count = rest[after:]
    tiles, slots = cd.shape[0], out.shape[1] // TILE
    for c in range(count.shape[0]):
        count[c] = 0

    @pl.loop(0, tiles)
    def _(i):
        label = cd[i]
        tile_of[label * tiles + count[label]] = i
        count[label] = count[label] + 1

    @pl.loop(0, ab.shape[0])
    def _(v):
        want = ab[v]

        @pl.when(first_of(ab, v) == v)
        def _():
            hot[...] = one_hot(hot.shape, jnp.where(labels[...] == want, rank[...], -1))
            used = jnp.clip(count[want] - skip, 0, slots)

            @pl.loop(0, (used + 1) // 2)
            def _(s):
                spans = []
                for k in range(2):
                    i = tile_of[jnp.minimum(want * tiles + skip + 2 * s + k, want * tiles + skip + used - 1)]
                    spans.append(t[:, pl.ds(pl.multiple_of(i * TILE, TILE), TILE)])
                rows_in = jnp.dot(hot[...], jnp.concatenate(spans, axis=1), preferred_element_type=jnp.float32)
                out[v, pl.ds(pl.multiple_of(s * 2 * TILE, 2 * TILE), 2 * TILE), :] = jnp.transpose(
                    rows_in
                ).astype(jnp.bfloat16)

            @pl.loop(2 * ((used + 1) // 2), slots)
            def _(s):
                out[v, pl.ds(pl.multiple_of(s * TILE, TILE), TILE), :] = jnp.zeros(
                    (TILE, out.shape[2]), jnp.bfloat16
                )


def first_of(ab, v):
    want = ab[v]
    first = jnp.int32(0)
    for a in reversed(range(ab.shape[0])):
        first = jnp.where(ab[a] == want, a, first)
    return first


def select(skip, slots, ab, cd, labels, rank, t, after):
    room = slots + slots % 2
    return pl.pallas_call(
        functools.partial(select_kernel, skip, len(after)),
        out_shape=jax.ShapeDtypeStruct((ab.shape[0], room * TILE, ROWS), t.dtype),
        in_specs=[SMEM, SMEM, VMEM, VMEM, VMEM] + [ANY] * len(after),
        out_specs=VMEM,
        scratch_shapes=[
            pltpu.VMEM((ROWS, t.shape[0]), jnp.bfloat16),
            pltpu.SMEM((8 * cd.shape[0],), jnp.int32),
            pltpu.SMEM((8,), jnp.int32),
        ],
        compiler_params=params(12),
        cost_estimate=cost(12.0),
        name="select_amplitudes",
    )(ab, cd, labels, rank, t, *after)


def product_kernel(blocks, nx, ny, where, ab, t, *rest):
    arrays, (keep, send, largest, acc) = rest[:-4], rest[-4:]
    x, y, core = where[0] // ny, where[0] % ny, where[2]
    part = acc.shape[0] // 4
    most = jnp.zeros((8, acc.shape[1]), jnp.float32)
    for b, block in enumerate(blocks):
        v = ((x + nx - b // 2) % nx) * ny + (y + b) % ny
        f = first_of(ab, v)
        first = 0
        for n, column, width in block:
            last = first + width
            p = jnp.dot(
                arrays[n][:, column : column + width],
                t[f, first:last, :],
                preferred_element_type=jnp.float32,
            )
            acc[...] = p if first == 0 else acc[...] + p
            first = last
        most = jnp.maximum(most, jnp.max(jnp.abs(acc[...]).reshape(-1, 8, acc.shape[1]), axis=0))
        for half in range(2):
            for out, c in ((keep, core), (send, 1 - core)):
                row = pl.multiple_of((2 * half + c) * part, part)
                out[v, half] = acc[pl.ds(row, part), :]
    largest[...] = jnp.full(largest.shape, jnp.max(most), jnp.float32)


def product(where, ab, t, blocks):
    shape = jax.ShapeDtypeStruct((t.shape[0], 2, TILE // 4, t.shape[2]), jnp.float32)
    arrays, places = [], []
    for block in blocks:
        places.append([])
        for v, column, width in block:
            if not any(v is a for a in arrays):
                arrays.append(v)
            places[-1].append(([v is a for a in arrays].index(True), column, width))
    return pl.pallas_call(
        functools.partial(product_kernel, places, lax.axis_size("x"), lax.axis_size("yl")),
        out_shape=[shape, shape, jax.ShapeDtypeStruct((8, TILE), jnp.float32)],
        in_specs=[SMEM] * 2 + [VMEM] * (1 + len(arrays)),
        out_specs=[VMEM, VMEM, VMEM],
        scratch_shapes=[pltpu.VMEM((TILE, t.shape[2]), jnp.float32)],
        compiler_params=params(12),
        cost_estimate=cost(1.6),
        name="product",
    )(where, ab, t, *arrays)


def combine_kernel(keep, got, a, b, out):
    top = (a[...] + b[...])[0:1, :]
    up, down = jnp.ones_like(top), jnp.ones_like(top)
    for bits in (64, 32, 8, 4, 2, 1):
        fits = top * (up * 2.0**bits) <= 2.0**15
        up = jnp.where(fits, up * 2.0**bits, up)
        down = jnp.where(fits, down * 2.0**-bits, down)
    lane = lax.broadcasted_iota(jnp.int32, top.shape, 1)
    parts = jnp.zeros_like(top)
    for i in range(SCALES):
        parts = jnp.where(lane == TILE - SCALES + i, jnp.maximum(down, 1.0 / STEP), parts)
        down = jnp.where(down < 1.0 / STEP, down * STEP, 1.0)
    up = jnp.concatenate([up, jnp.where(lane < TILE - SCALES, up, 0.0)], axis=1)
    parts = jnp.concatenate([jnp.zeros_like(top), parts], axis=1)
    for v in range(keep.shape[0]):
        for y in range(keep.shape[1]):
            out[v * keep.shape[1] + y] = (keep[v, y] + got[v, y]) * up + parts


def combine(keep, got, a, b):
    return pl.pallas_call(
        combine_kernel,
        out_shape=jax.ShapeDtypeStruct((keep.shape[0] * keep.shape[1],) + keep.shape[2:], jnp.float32),
        in_specs=[VMEM] * 4,
        out_specs=VMEM,
        compiler_params=params(6),
        cost_estimate=cost(1.2),
        name="combine",
    )(keep, got, a, b)


def spread_kernel(where, ab, labels, rank, spots, parts, own, send):
    total = jnp.zeros(parts.shape[1:], jnp.float32)
    for z in range(parts.shape[0]):
        part = parts[z]
        down = part[0:1, ROWS - SCALES : ROWS - SCALES + 1]
        for i in range(1, SCALES):
            down *= part[0:1, ROWS - SCALES + i : ROWS - SCALES + i + 1]
        total += part * down
    high = total.astype(jnp.bfloat16)
    rest = total - high.astype(jnp.float32)
    middle = rest.astype(jnp.bfloat16)
    low = (rest - middle.astype(jnp.float32)).astype(jnp.bfloat16)
    split = jnp.concatenate([high, middle, low], axis=0)
    n = total.shape[0]

    def placed(spot):
        x = jnp.dot(split, one_hot((total.shape[1], spot.shape[1]), spot), preferred_element_type=jnp.float32)
        return x[:n] + (x[n : 2 * n] + x[2 * n :])

    for o in range(0, send.shape[0], 2):
        x = placed(spots[:, o * TILE : (o + 2) * TILE])
        send[o] = x[:, :TILE]
        send[o + 1] = x[:, TILE:]
    mine = ab[where[1]]
    for k in range(0, own.shape[1], 2 * TILE):
        span = slice(k, k + 2 * TILE)
        own[:, span] = placed(jnp.where(labels[:, span] == mine, rank[:, span], -1))


def spread(where, ab, labels, rank, spots, parts):
    return pl.pallas_call(
        spread_kernel,
        out_shape=[
            jax.ShapeDtypeStruct((parts.shape[1], labels.shape[1]), jnp.float32),
            jax.ShapeDtypeStruct((spots.shape[1] // TILE, parts.shape[1], TILE), jnp.float32),
        ],
        in_specs=[SMEM, SMEM] + [VMEM] * 4,
        out_specs=[VMEM, VMEM],
        compiler_params=params(6),
        cost_estimate=cost(1.7),
        name="spread",
    )(where, ab, labels, rank, spots, parts)


def finish_kernel(own, got, out, turned):
    local, orbitals, width = turned.shape
    for o in range(got.shape[0]):
        x = jnp.transpose(got[o])
        for i in range(local):
            turned[i, o * local : (o + 1) * local, :] = x[i * local : (i + 1) * local, :]
    for i in range(local):
        mine = own[:, i * orbitals : (i + 1) * orbitals]
        out[i * width : (i + 1) * width, :] = (2.0 * mine - jnp.transpose(turned[i])).astype(jnp.bfloat16)


def finish(own, got, local, orbitals):
    width = own.shape[0]
    return pl.pallas_call(
        finish_kernel,
        out_shape=jax.ShapeDtypeStruct((local * width, orbitals), jnp.bfloat16),
        in_specs=[VMEM, VMEM],
        out_specs=VMEM,
        scratch_shapes=[pltpu.VMEM((local, orbitals, width), jnp.float32)],
        compiler_params=params(4),
        cost_estimate=cost(0.4),
        name="finish",
    )(own, got)


def join_kernel(after, *refs):
    ins, out = refs[after:-1], refs[-1]
    first = 0
    for v in ins:
        out[:, first : first + v.shape[1]] = v[...]
        first += v.shape[1]


def join(blocks, after):
    return pl.pallas_call(
        functools.partial(join_kernel, len(after)),
        out_shape=jax.ShapeDtypeStruct(
            (blocks[0].shape[0], sum(v.shape[1] for v in blocks)), blocks[0].dtype
        ),
        in_specs=[ANY] * len(after) + [VMEM] * len(blocks),
        out_specs=VMEM,
        compiler_params=params(6),
        cost_estimate=cost(0.4),
        name="join",
    )(*after, *blocks)


def gather(pieces):
    nx, ny = lax.axis_size("x"), lax.axis_size("yl")
    swap = shifted("yl", ny, 1)
    up, down = shifted("x", nx, 1), shifted("x", nx, nx - 1)
    first, rest = pieces[0], pieces[1:]
    width = first.shape[1]
    partner = swap(first)
    early = [[shifted("x", nx, step)(v) for v in rest] for step in range(1, nx)]
    mine = {1: up(first), nx - 1: down(first)}
    other = {1: up(partner), nx - 1: down(partner)}
    for step in range(2, nx - 1):
        mine[step] = up(mine[step - 1])
        other[nx - step] = down(other[nx - step + 1])
    blocks = [[(first, 0, width)], [(partner, 0, width)]]
    for step in range(1, nx):
        blocks += [[(mine[step], 0, width)], [(other[step], 0, width)]]
    passed = []
    if rest:
        through = [rest[0]] + [v[0] for v in early]
        passed = [join(through, [partner])]
        back = swap(passed[0])
        step = rest[0].shape[1]
        for k, v in enumerate(through):
            blocks[2 * k].append((v, 0, step))
            blocks[2 * k + 1].append((back, k * step, step))
    return blocks, passed


def dense(amplitudes, integrals, occ_irrep, ab_irrep, cd_irrep):
    rows, cols = amplitudes.shape
    orbitals = occ_irrep.shape[0]
    groups = lax.axis_size("x") * lax.axis_size("yl")
    local = orbitals // groups
    me = lax.axis_index("x") * lax.axis_size("yl") + lax.axis_index("yl")
    blocks = lax.all_to_all(
        jnp.broadcast_to(integrals, (groups,) + integrals.shape), ("x", "yl"), 0, 0, tiled=True
    )
    mine = lax.dynamic_slice_in_dim(occ_irrep, me * local, local)
    pair = jnp.bitwise_xor(mine[:, None], occ_irrep[None, :]).reshape(rows)
    col = jnp.repeat(cd_irrep, TILE)
    masked_t = jnp.where(pair[:, None] == col[None, :], amplitudes, 0)
    masked_v = jnp.where(ab_irrep[:, None, None] == col[None, None, :], blocks, 0)
    part = lax.dot_general(
        masked_v.reshape(-1, cols), masked_t, (((1,), (1,)), ((), ())), preferred_element_type=jnp.float32
    )
    part = part.reshape(groups * 4, TILE // 4, rows)
    part = lax.all_to_all(part, ("vir", "yh", "core"), 0, 0, tiled=True).sum(0)
    own = part.reshape(TILE // 4, local, groups, local).transpose(2, 0, 1, 3)
    got = lax.all_to_all(own, ("x", "yl"), 0, 0, tiled=True)
    out = 2.0 * own.transpose(2, 0, 3, 1) - got.transpose(3, 0, 2, 1)
    return out.reshape(local, orbitals, TILE // 4).astype(jnp.bfloat16)


def per_device(amplitudes, integrals, occ_irrep, ab_irrep, cd_irrep):
    groups = lax.axis_size("x") * lax.axis_size("yl")
    orbitals = occ_irrep.shape[0]
    rows = amplitudes.shape[0]
    me = lax.axis_index("x") * lax.axis_size("yl") + lax.axis_index("yl")
    where = jnp.stack([me, lax.axis_index("vir"), lax.axis_index("core")]).astype(jnp.int32)
    tiles = cd_irrep.shape[0]

    def partial_sums(skip, slots, found, blocks, passed):
        selected = select(skip, slots, ab_irrep, cd_irrep, *found[:2], amplitudes, passed)
        return product(where, ab_irrep, selected, blocks)

    done = sum(FIRST)
    more, *packed = pack(0, FIRST, where, ab_irrep, cd_irrep, integrals)
    blocks, passed = gather(packed)
    found = ranks(where, occ_irrep, ab_irrep, rows, groups, [])
    sums = partial_sums(0, done, found, blocks, passed)

    def rest(sums, v, found):
        _, packed = pack(done, (tiles - done,), where, ab_irrep, cd_irrep, v)
        blocks, _ = gather([packed])
        return jax.tree.map(jnp.add, list(sums), list(partial_sums(done, tiles - done, found, blocks, [])))

    keep, send, largest = lax.cond(
        more[0] > 0, rest, lambda sums, v, found: list(sums), list(sums), integrals, found
    )
    labels, rank, spots, over = found
    other = shifted("core", 2, 1)
    part = combine(keep, other(send), largest, other(largest)).astype(jnp.float16)
    part = lax.all_to_all(part, ("vir", "yh"), 0, 0, tiled=True).astype(jnp.float32)
    own, send = spread(where, ab_irrep, labels, rank, spots, part)
    got = lax.all_to_all(send, ("x", "yl"), 0, 0, tiled=True)
    out = lax.cond(
        over[0] > 0,
        lambda own, got, *a: jnp.swapaxes(dense(*a), 1, 2).reshape(-1, orbitals),
        lambda own, got, *a: finish(own, got, rows // orbitals, orbitals),
        *(own, got, amplitudes, integrals, occ_irrep, ab_irrep, cd_irrep),
    )
    return jnp.swapaxes(out.reshape(rows // orbitals, -1, orbitals), 1, 2)


def solution(mesh):
    occ, vir, con = (mesh.shape[a] for a in ("occ", "vir", "con"))
    split = Mesh(
        mesh.devices.reshape(occ // 2, 2, vir, 2, con // 2), ("x", "yl", "vir", "yh", "core")
    )
    cd = ("vir", "yh", "core")
    return jax.shard_map(
        per_device,
        mesh=split,
        in_specs=(P(("x", "yl"), cd), P(("x", "yl"), cd), P(), P(), P(cd)),
        out_specs=P(("x", "yl"), None, cd),
        check_vma=False,
    )
```

```python
import functools

import jax
import jax.numpy as jnp
from jax import lax
from jax.experimental import pallas as pl
from jax.experimental.pallas import tpu as pltpu
from jax.sharding import Mesh, PartitionSpec as P

TILE = 128
ROWS = 256
SCALES = 8
STEP = 2.0**14
FIRST = (7, 4)
MIB = 1 << 20
SMEM = pl.BlockSpec(memory_space=pltpu.SMEM)
VMEM = pl.BlockSpec(memory_space=pltpu.VMEM)
ANY = pl.BlockSpec(memory_space=pl.ANY)


def shifted(axis, size, step):
    return lambda a: lax.ppermute(a, axis, [(i, (i + step) % size) for i in range(size)])


def cost(us):
    return pl.CostEstimate(flops=int(us * 1.1e9), bytes_accessed=0, transcendentals=0)


def params(mib):
    return pltpu.CompilerParams(vmem_limit_bytes=mib * MIB)


def pack_kernel(skip, where, ab, cd, v, more, *rest):
    outs, count = rest[:-1], rest[-1]
    mine = ab[where[0]]
    for c in range(count.shape[0]):
        count[c] = 0

    @pl.loop(0, cd.shape[0])
    def _(t):
        label = cd[t]
        slot = count[label] - skip
        count[label] = count[label] + 1

        @pl.when(label == mine)
        def _():
            tile = v[:, pl.ds(pl.multiple_of(t * TILE, TILE), TILE)]
            first = 0
            for out in outs:
                place = slot - first
                slots = out.shape[1] // TILE

                @pl.when((place >= 0) & (place < slots))
                def _():
                    out[:, pl.ds(pl.multiple_of(place * TILE, TILE), TILE)] = tile

                first += slots

    first = skip
    for out in outs:
        slots = out.shape[1] // TILE

        @pl.loop(jnp.clip(count[mine] - first, 0, slots), slots)
        def _(slot):
            out[:, pl.ds(pl.multiple_of(slot * TILE, TILE), TILE)] = jnp.zeros((v.shape[0], TILE), v.dtype)

        first += slots
    most = count[ab[0]]
    for a in range(1, ab.shape[0]):
        most = jnp.maximum(most, count[ab[a]])
    more[0] = (most > first).astype(jnp.int32)


def pack(skip, pieces, where, ab, cd, v):
    return pl.pallas_call(
        functools.partial(pack_kernel, skip),
        out_shape=[jax.ShapeDtypeStruct((1,), jnp.int32)]
        + [jax.ShapeDtypeStruct((v.shape[0], slots * TILE), v.dtype) for slots in pieces],
        in_specs=[SMEM, SMEM, SMEM, VMEM],
        out_specs=[SMEM] + [VMEM] * len(pieces),
        scratch_shapes=[pltpu.SMEM((8,), jnp.int32)],
        compiler_params=params(4),
        cost_estimate=cost(2.0),
        name="pack_integrals",
    )(where, ab, cd, v)


def one_hot(shape, spot):
    match = lax.broadcasted_iota(jnp.int32, shape, 0) == spot
    return match.astype(jnp.float32).astype(jnp.bfloat16)


def rank_kernel(after, where, occ, ab, occ_row, *rest):
    labels, rank, spots, over = rest[after:]
    orbitals, rows = occ_row.shape[1], labels.shape[1]
    local = rows // orbitals
    irreps, abt = 8, ab.shape[0]
    me, mine = where[0], ab[where[1]]
    for i in range(local):
        labels[:, i * orbitals : (i + 1) * orbitals] = occ_row[...] ^ occ[me * local + i]

    label = labels[...]
    is_label = lax.broadcasted_iota(jnp.int32, (irreps, rows), 0) == label
    marks = is_label.astype(jnp.float32).astype(jnp.bfloat16)

    @pl.loop(0, rows // TILE)
    def _(k):
        first = pl.multiple_of(k * TILE, TILE)
        shape = (rows, TILE)
        before = lax.broadcasted_iota(jnp.int32, shape, 0) < first + lax.broadcasted_iota(
            jnp.int32, shape, 1
        )
        ahead = jnp.dot(
            marks, before.astype(jnp.float32).astype(jnp.bfloat16), preferred_element_type=jnp.float32
        )
        own = lax.broadcasted_iota(jnp.int32, (irreps, TILE), 0) == labels[:, pl.ds(first, TILE)]
        rank[:, pl.ds(first, TILE)] = jnp.sum(
            jnp.where(own, ahead, 0.0), axis=0, keepdims=True
        ).astype(jnp.int32)

    column = lax.broadcasted_iota(jnp.int32, (abt, orbitals), 0)
    partner = occ_row[...]
    want = jnp.zeros((abt, orbitals), jnp.int32)
    for v in range(abt):
        want = jnp.where(column == v, ab[v], want)
    want = want ^ partner
    of_irrep = lax.broadcasted_iota(jnp.int32, (irreps, orbitals), 0) == partner
    count = jnp.sum(of_irrep.astype(jnp.float32), axis=1, keepdims=True)
    met = jnp.zeros((abt, orbitals), jnp.float32)
    for c in range(irreps):
        met = jnp.where(want == c, count[c : c + 1, :], met)
    shape = (orbitals, TILE)
    group = lax.broadcasted_iota(jnp.int32, shape, 0) // local == lax.broadcasted_iota(jnp.int32, shape, 1)
    held = jnp.dot(
        met.astype(jnp.bfloat16),
        group.astype(jnp.float32).astype(jnp.bfloat16),
        preferred_element_type=jnp.float32,
    )
    over[0] = (jnp.max(held) > ROWS - SCALES).astype(jnp.int32)

    which = lax.broadcasted_iota(jnp.int32, (8, rows), 0)
    place = rank[...]
    values = jnp.where(
        which == 0, label, jnp.where(which == 1, place % 256, jnp.where(which == 2, place // 256, 0))
    )
    values = values.astype(jnp.float32).astype(jnp.bfloat16)

    @pl.loop(0, spots.shape[1] // TILE)
    def _(owner):
        lane = lax.broadcasted_iota(jnp.int32, (1, TILE), 1)
        j, i = lane // local, lane % local
        source = jnp.where(j < local, i * orbitals + owner * local + j, -1)
        moved = jnp.dot(
            values, one_hot((rows, TILE), source), preferred_element_type=jnp.float32
        ).astype(jnp.int32)
        here = (moved[0:1] == mine) & (j < local)
        spots[:, pl.ds(pl.multiple_of(owner * TILE, TILE), TILE)] = jnp.where(
            here, moved[1:2] + 256 * moved[2:3], -1
        )


def ranks(where, occ, ab, rows, groups, after):
    return pl.pallas_call(
        functools.partial(rank_kernel, len(after)),
        out_shape=[
            jax.ShapeDtypeStruct((1, rows), jnp.int32),
            jax.ShapeDtypeStruct((1, rows), jnp.int32),
            jax.ShapeDtypeStruct((1, groups * TILE), jnp.int32),
            jax.ShapeDtypeStruct((1,), jnp.int32),
        ],
        in_specs=[SMEM, SMEM, SMEM, VMEM] + [ANY] * len(after),
        out_specs=[VMEM, VMEM, VMEM, SMEM],
        compiler_params=params(4),
        cost_estimate=cost(3.3),
        name="ranks",
    )(where, occ, ab, occ.reshape(1, -1), *after)


def select_kernel(skip, after, ab, cd, labels, rank, t, *rest):
    out, hot, tile_of, count = rest[after:]
    tiles, slots = cd.shape[0], out.shape[1] // TILE
    for c in range(count.shape[0]):
        count[c] = 0

    @pl.loop(0, tiles)
    def _(i):
        label = cd[i]
        tile_of[label * tiles + count[label]] = i
        count[label] = count[label] + 1

    @pl.loop(0, ab.shape[0])
    def _(v):
        want = ab[v]

        @pl.when(first_of(ab, v) == v)
        def _():
            hot[...] = one_hot(hot.shape, jnp.where(labels[...] == want, rank[...], -1))
            used = jnp.clip(count[want] - skip, 0, slots)

            @pl.loop(0, (used + 1) // 2)
            def _(s):
                spans = []
                for k in range(2):
                    i = tile_of[jnp.minimum(want * tiles + skip + 2 * s + k, want * tiles + skip + used - 1)]
                    spans.append(t[:, pl.ds(pl.multiple_of(i * TILE, TILE), TILE)])
                rows_in = jnp.dot(hot[...], jnp.concatenate(spans, axis=1), preferred_element_type=jnp.float32)
                out[v, pl.ds(pl.multiple_of(s * 2 * TILE, 2 * TILE), 2 * TILE), :] = jnp.transpose(
                    rows_in
                ).astype(jnp.bfloat16)

            @pl.loop(2 * ((used + 1) // 2), slots)
            def _(s):
                out[v, pl.ds(pl.multiple_of(s * TILE, TILE), TILE), :] = jnp.zeros(
                    (TILE, out.shape[2]), jnp.bfloat16
                )


def first_of(ab, v):
    want = ab[v]
    first = jnp.int32(0)
    for a in reversed(range(ab.shape[0])):
        first = jnp.where(ab[a] == want, a, first)
    return first


def select(skip, slots, ab, cd, labels, rank, t, after):
    room = slots + slots % 2
    return pl.pallas_call(
        functools.partial(select_kernel, skip, len(after)),
        out_shape=jax.ShapeDtypeStruct((ab.shape[0], room * TILE, ROWS), t.dtype),
        in_specs=[SMEM, SMEM, VMEM, VMEM, VMEM] + [ANY] * len(after),
        out_specs=VMEM,
        scratch_shapes=[
            pltpu.VMEM((ROWS, t.shape[0]), jnp.bfloat16),
            pltpu.SMEM((8 * cd.shape[0],), jnp.int32),
            pltpu.SMEM((8,), jnp.int32),
        ],
        compiler_params=params(12),
        cost_estimate=cost(12.0),
        name="select_amplitudes",
    )(ab, cd, labels, rank, t, *after)


def product_kernel(blocks, nx, ny, where, ab, t, *rest):
    arrays, (keep, send, largest, acc) = rest[:-4], rest[-4:]
    x, y, core = where[0] // ny, where[0] % ny, where[2]
    part = acc.shape[0] // 4
    most = jnp.zeros((8, acc.shape[1]), jnp.float32)
    for b, block in enumerate(blocks):
        v = ((x + nx - b // 2) % nx) * ny + (y + b) % ny
        f = first_of(ab, v)
        first = 0
        for n, column, width in block:
            last = first + width
            p = jnp.dot(
                arrays[n][:, column : column + width],
                t[f, first:last, :],
                preferred_element_type=jnp.float32,
            )
            acc[...] = p if first == 0 else acc[...] + p
            first = last
        most = jnp.maximum(most, jnp.max(jnp.abs(acc[...]).reshape(-1, 8, acc.shape[1]), axis=0))
        for half in range(2):
            for out, c in ((keep, core), (send, 1 - core)):
                row = pl.multiple_of((2 * half + c) * part, part)
                out[v, half] = acc[pl.ds(row, part), :]
    top = jnp.full(largest.shape, jnp.max(most), jnp.float32)
    largest[...] = top
    lane = lax.broadcasted_iota(jnp.int32, top.shape, 1)
    spare = send[send.shape[0] - 1, 1, 0:8, ROWS - TILE :]
    send[send.shape[0] - 1, 1, 0:8, ROWS - TILE :] = jnp.where(lane < TILE - SCALES, spare, top)


def product(where, ab, t, blocks):
    shape = jax.ShapeDtypeStruct((t.shape[0], 2, TILE // 4, t.shape[2]), jnp.float32)
    arrays, places = [], []
    for block in blocks:
        places.append([])
        for v, column, width in block:
            if not any(v is a for a in arrays):
                arrays.append(v)
            places[-1].append(([v is a for a in arrays].index(True), column, width))
    return pl.pallas_call(
        functools.partial(product_kernel, places, lax.axis_size("x"), lax.axis_size("yl")),
        out_shape=[shape, shape, jax.ShapeDtypeStruct((8, TILE), jnp.float32)],
        in_specs=[SMEM] * 2 + [VMEM] * (1 + len(arrays)),
        out_specs=[VMEM, VMEM, VMEM],
        scratch_shapes=[pltpu.VMEM((TILE, t.shape[2]), jnp.float32)],
        compiler_params=params(12),
        cost_estimate=cost(1.6),
        name="product",
    )(where, ab, t, *arrays)


def combine_kernel(keep, got, a, out):
    top = a[0:1, :] + got[got.shape[0] - 1, 1, 0:1, ROWS - TILE :][:, TILE - 1 :]
    up, down = jnp.ones_like(top), jnp.ones_like(top)
    for bits in (64, 32, 8, 4, 2, 1):
        fits = top * (up * 2.0**bits) <= 2.0**15
        up = jnp.where(fits, up * 2.0**bits, up)
        down = jnp.where(fits, down * 2.0**-bits, down)
    lane = lax.broadcasted_iota(jnp.int32, top.shape, 1)
    parts = jnp.zeros_like(top)
    for i in range(SCALES):
        parts = jnp.where(lane == TILE - SCALES + i, jnp.maximum(down, 1.0 / STEP), parts)
        down = jnp.where(down < 1.0 / STEP, down * STEP, 1.0)
    up = jnp.concatenate([up, jnp.where(lane < TILE - SCALES, up, 0.0)], axis=1)
    parts = jnp.concatenate([jnp.zeros_like(top), parts], axis=1)
    for v in range(keep.shape[0]):
        for y in range(keep.shape[1]):
            out[v * keep.shape[1] + y] = (keep[v, y] + got[v, y]) * up + parts


def combine(keep, got, a):
    return pl.pallas_call(
        combine_kernel,
        out_shape=jax.ShapeDtypeStruct((keep.shape[0] * keep.shape[1],) + keep.shape[2:], jnp.float32),
        in_specs=[VMEM] * 3,
        out_specs=VMEM,
        compiler_params=params(6),
        cost_estimate=cost(1.2),
        name="combine",
    )(keep, got, a)


def spread_kernel(where, ab, labels, rank, spots, parts, own, send):
    total = jnp.zeros(parts.shape[1:], jnp.float32)
    for z in range(parts.shape[0]):
        part = parts[z]
        down = part[0:1, ROWS - SCALES : ROWS - SCALES + 1]
        for i in range(1, SCALES):
            down *= part[0:1, ROWS - SCALES + i : ROWS - SCALES + i + 1]
        total += part * down
    high = total.astype(jnp.bfloat16)
    rest = total - high.astype(jnp.float32)
    middle = rest.astype(jnp.bfloat16)
    low = (rest - middle.astype(jnp.float32)).astype(jnp.bfloat16)
    split = jnp.concatenate([high, middle, low], axis=0)
    n = total.shape[0]

    def placed(spot):
        x = jnp.dot(split, one_hot((total.shape[1], spot.shape[1]), spot), preferred_element_type=jnp.float32)
        return x[:n] + (x[n : 2 * n] + x[2 * n :])

    for o in range(0, send.shape[0], 2):
        x = placed(spots[:, o * TILE : (o + 2) * TILE])
        send[o] = x[:, :TILE]
        send[o + 1] = x[:, TILE:]
    mine = ab[where[1]]
    for k in range(0, own.shape[1], 2 * TILE):
        span = slice(k, k + 2 * TILE)
        own[:, span] = placed(jnp.where(labels[:, span] == mine, rank[:, span], -1))


def spread(where, ab, labels, rank, spots, parts):
    return pl.pallas_call(
        spread_kernel,
        out_shape=[
            jax.ShapeDtypeStruct((parts.shape[1], labels.shape[1]), jnp.float32),
            jax.ShapeDtypeStruct((spots.shape[1] // TILE, parts.shape[1], TILE), jnp.float32),
        ],
        in_specs=[SMEM, SMEM] + [VMEM] * 4,
        out_specs=[VMEM, VMEM],
        compiler_params=params(6),
        cost_estimate=cost(1.7),
        name="spread",
    )(where, ab, labels, rank, spots, parts)


def finish_kernel(own, got, out, turned):
    local, orbitals, width = turned.shape
    for o in range(got.shape[0]):
        x = jnp.transpose(got[o])
        for i in range(local):
            turned[i, o * local : (o + 1) * local, :] = x[i * local : (i + 1) * local, :]
    for i in range(local):
        mine = own[:, i * orbitals : (i + 1) * orbitals]
        out[i * width : (i + 1) * width, :] = (2.0 * mine - jnp.transpose(turned[i])).astype(jnp.bfloat16)


def finish(own, got, local, orbitals):
    width = own.shape[0]
    return pl.pallas_call(
        finish_kernel,
        out_shape=jax.ShapeDtypeStruct((local * width, orbitals), jnp.bfloat16),
        in_specs=[VMEM, VMEM],
        out_specs=VMEM,
        scratch_shapes=[pltpu.VMEM((local, orbitals, width), jnp.float32)],
        compiler_params=params(4),
        cost_estimate=cost(0.4),
        name="finish",
    )(own, got)


def join_kernel(after, *refs):
    ins, out = refs[after:-1], refs[-1]
    first = 0
    for v in ins:
        out[:, first : first + v.shape[1]] = v[...]
        first += v.shape[1]


def join(blocks, after):
    return pl.pallas_call(
        functools.partial(join_kernel, len(after)),
        out_shape=jax.ShapeDtypeStruct(
            (blocks[0].shape[0], sum(v.shape[1] for v in blocks)), blocks[0].dtype
        ),
        in_specs=[ANY] * len(after) + [VMEM] * len(blocks),
        out_specs=VMEM,
        compiler_params=params(6),
        cost_estimate=cost(0.4),
        name="join",
    )(*after, *blocks)


def gather(pieces):
    nx, ny = lax.axis_size("x"), lax.axis_size("yl")
    swap = shifted("yl", ny, 1)
    up, down = shifted("x", nx, 1), shifted("x", nx, nx - 1)
    first, rest = pieces[0], pieces[1:]
    width = first.shape[1]
    partner = swap(first)
    early = [[shifted("x", nx, step)(v) for v in rest] for step in range(1, nx)]
    mine = {1: up(first), nx - 1: down(first)}
    other = {1: up(partner), nx - 1: down(partner)}
    for step in range(2, nx - 1):
        mine[step] = up(mine[step - 1])
        other[nx - step] = down(other[nx - step + 1])
    blocks = [[(first, 0, width)], [(partner, 0, width)]]
    for step in range(1, nx):
        blocks += [[(mine[step], 0, width)], [(other[step], 0, width)]]
    passed = []
    if rest:
        through = [rest[0]] + [v[0] for v in early]
        passed = [join(through, [partner])]
        back = swap(passed[0])
        step = rest[0].shape[1]
        for k, v in enumerate(through):
            blocks[2 * k].append((v, 0, step))
            blocks[2 * k + 1].append((back, k * step, step))
    return blocks, passed


def dense(amplitudes, integrals, occ_irrep, ab_irrep, cd_irrep):
    rows, cols = amplitudes.shape
    orbitals = occ_irrep.shape[0]
    groups = lax.axis_size("x") * lax.axis_size("yl")
    local = orbitals // groups
    me = lax.axis_index("x") * lax.axis_size("yl") + lax.axis_index("yl")
    blocks = lax.all_to_all(
        jnp.broadcast_to(integrals, (groups,) + integrals.shape), ("x", "yl"), 0, 0, tiled=True
    )
    mine = lax.dynamic_slice_in_dim(occ_irrep, me * local, local)
    pair = jnp.bitwise_xor(mine[:, None], occ_irrep[None, :]).reshape(rows)
    col = jnp.repeat(cd_irrep, TILE)
    masked_t = jnp.where(pair[:, None] == col[None, :], amplitudes, 0)
    masked_v = jnp.where(ab_irrep[:, None, None] == col[None, None, :], blocks, 0)
    part = lax.dot_general(
        masked_v.reshape(-1, cols), masked_t, (((1,), (1,)), ((), ())), preferred_element_type=jnp.float32
    )
    part = part.reshape(groups * 4, TILE // 4, rows)
    part = lax.all_to_all(part, ("vir", "yh", "core"), 0, 0, tiled=True).sum(0)
    own = part.reshape(TILE // 4, local, groups, local).transpose(2, 0, 1, 3)
    got = lax.all_to_all(own, ("x", "yl"), 0, 0, tiled=True)
    out = 2.0 * own.transpose(2, 0, 3, 1) - got.transpose(3, 0, 2, 1)
    return out.reshape(local, orbitals, TILE // 4).astype(jnp.bfloat16)


def per_device(amplitudes, integrals, occ_irrep, ab_irrep, cd_irrep):
    groups = lax.axis_size("x") * lax.axis_size("yl")
    orbitals = occ_irrep.shape[0]
    rows = amplitudes.shape[0]
    me = lax.axis_index("x") * lax.axis_size("yl") + lax.axis_index("yl")
    where = jnp.stack([me, lax.axis_index("vir"), lax.axis_index("core")]).astype(jnp.int32)
    tiles = cd_irrep.shape[0]

    def partial_sums(skip, slots, found, blocks, passed):
        selected = select(skip, slots, ab_irrep, cd_irrep, *found[:2], amplitudes, passed)
        return product(where, ab_irrep, selected, blocks)

    done = sum(FIRST)
    more, *packed = pack(0, FIRST, where, ab_irrep, cd_irrep, integrals)
    blocks, passed = gather(packed)
    found = ranks(where, occ_irrep, ab_irrep, rows, groups, [])
    sums = partial_sums(0, done, found, blocks, passed)

    def rest(sums, v, found):
        _, packed = pack(done, (tiles - done,), where, ab_irrep, cd_irrep, v)
        blocks, _ = gather([packed])
        return jax.tree.map(jnp.add, list(sums), list(partial_sums(done, tiles - done, found, blocks, [])))

    keep, send, largest = lax.cond(
        more[0] > 0, rest, lambda sums, v, found: list(sums), list(sums), integrals, found
    )
    labels, rank, spots, over = found
    other = shifted("core", 2, 1)
    part = combine(keep, other(send), largest).astype(jnp.float16)
    part = lax.all_to_all(part, ("vir", "yh"), 0, 0, tiled=True).astype(jnp.float32)
    own, send = spread(where, ab_irrep, labels, rank, spots, part)
    got = lax.all_to_all(send, ("x", "yl"), 0, 0, tiled=True)
    out = lax.cond(
        over[0] > 0,
        lambda own, got, *a: jnp.swapaxes(dense(*a), 1, 2).reshape(-1, orbitals),
        lambda own, got, *a: finish(own, got, rows // orbitals, orbitals),
        *(own, got, amplitudes, integrals, occ_irrep, ab_irrep, cd_irrep),
    )
    return jnp.swapaxes(out.reshape(rows // orbitals, -1, orbitals), 1, 2)


def solution(mesh):
    occ, vir, con = (mesh.shape[a] for a in ("occ", "vir", "con"))
    split = Mesh(
        mesh.devices.reshape(occ // 2, 2, vir, 2, con // 2), ("x", "yl", "vir", "yh", "core")
    )
    cd = ("vir", "yh", "core")
    return jax.shard_map(
        per_device,
        mesh=split,
        in_specs=(P(("x", "yl"), cd), P(("x", "yl"), cd), P(), P(), P(cd)),
        out_specs=P(("x", "yl"), None, cd),
        check_vma=False,
    )
```
